512 devices in a mesh: rows: 32 (over y, x, core), heads: 16 (over z).
Axes of the slice: x: 4, y: 4, z: 16, core: 2. Of those that a mesh axis runs over, the one named last changes fastest.
Arguments:
- pixels: float32 [8192, 768], P('rows'), may hold values from -6 to 6
- perturbation: float32 [8192, 768], P('rows'), may hold values from -0.6 to 0.6
- segment_ids: int32 [32, 256], P('rows'), may hold values from 0 to 3, never falling along the last dimension, each value on 1 to 128 neighbouring positions
- ball_radius: float32 [32, 4], P('rows'), may hold values from 0.05 to 0.4
- w_embed: bfloat16 [768, 1024], replicated, may hold values from -0.21875 to 0.21875
- gain_attn: float32 [1024], replicated, may hold values from 0.5 to 1.5
- w_qkv: bfloat16 [1024, 3, 1024], P('rows', None, 'heads'), may hold values from -0.1875 to 0.1875
- w_out: bfloat16 [1024, 1024], P('heads', 'rows'), may hold values from -0.1875 to 0.1875
- gain_mlp: float32 [1024], replicated, may hold values from 0.5 to 1.5
- w_up: bfloat16 [1024, 4096], P('rows', 'heads'), may hold values from -0.1875 to 0.1875
- w_down: bfloat16 [4096, 1024], P('heads', 'rows'), may hold values from -0.09375 to 0.09375
- out_grad: bfloat16 [8192, 1024], P('rows'), may hold values from -6 to 6
Outputs:
- block_out: bfloat16 [8192, 1024], P('rows')
- new_perturbation: float32 [8192, 768], P('rows')
The draws below stay inside these ranges and needn't reach their ends.
Inputs may be any that keep to these rules, and one draw needn't show every extreme that they name: `segment_ids`: each pack numbers its images 0 to 3 in order along the pack; each image has 1 to 128 patches and some image of every pack has exactly 128.
All inputs are finite; a program needn't handle non-finite values.
Results may differ from the reference program's by a relative error of at most 0.019.
Values may be sent and summed in bfloat16 or wider, within the bound.
No kernel may reach another device: no remote copies, remote signals or barrier semaphores. Data moves between devices by JAX's collectives and lax.ppermute only.
A program may use at most 64 MiB of HBM per device.

```python
import math
import jax
import jax.numpy as jnp
import numpy as np
from jax import lax

D = 1024
HEADS = 16
FF = 4096
PATCH = 768
TOK_ROW = 256
SEGS = 4
PACKS = 32
TOKENS = 8192
N_ROWS = 32
N_HEADS = 16


def block_scale(rng, extent, shards, low, largest):
    level = 1.0
    for position, shards_of in shards:
        steps = jax.random.uniform(jax.random.fold_in(jax.random.fold_in(rng, 6), position), (shards_of,), jnp.float32, low / len(shards), largest / len(shards))
        level = level * jnp.repeat(jnp.exp(steps), extent[position] // shards_of).reshape((-1,) + (1,) * (len(extent) - 1 - position))
    return level


def length_profile(amount, total, reach, lean):
    portions = [(1 << 20) // math.isqrt(grade ** lean) + 1 for grade in range(2, amount + 1)]
    surplus, holding = total - reach - (amount - 1), [1] * (amount - 1)
    while surplus > 0:
        free = [i for i in range(amount - 1) if holding[i] < reach]
        pool, remaining = sum([portions[i] for i in free]), surplus
        for i in free:
            addition = min(reach - holding[i], max(1, remaining * portions[i] // pool), surplus)
            holding[i] = holding[i] + addition
            surplus = surplus - addition
    return np.array([reach] + holding)


def uneven(rng, amount, total, bound, lean):
    if amount == 2:
        one = jax.random.randint(rng, (), max(1, total - bound), min(bound, total - 1) + 1)
        return jnp.stack([one, total - one])
    lengths = jnp.asarray(length_profile(amount, total, bound, lean), jnp.int32)
    pairs = (amount - 1) // 2
    source_of, sink = lengths[1:1 + 2 * pairs:2], lengths[2:2 + 2 * pairs:2]
    room = jnp.minimum(source_of - 1, bound - sink)
    passed = jax.random.randint(jax.random.fold_in(rng, 1), (pairs,), 0, 1 << 20) % (room + 1)
    lengths = lengths.at[1:1 + 2 * pairs:2].set(source_of - passed).at[2:2 + 2 * pairs:2].set(sink + passed)
    return lengths[jax.random.permutation(jax.random.fold_in(rng, 2), amount)]


def centred(stream_key, dims, deviation, bound, shards=(), held_as=jnp.bfloat16):
    factor_of = block_scale(stream_key, dims, shards, -0.22, 0.18) if shards else 1.0
    drawn = jax.random.normal(stream_key, dims, jnp.float32) * deviation * factor_of
    return jnp.minimum(jnp.maximum(drawn, -bound), bound).astype(held_as)


def setup_inputs(seed: int = 0) -> dict:
    key_list = jax.random.split(jax.random.key(seed), 13)
    pixels = centred(key_list[0], (TOKENS, PATCH), 1.0, 6.0, ((0, 32),), jnp.float32)
    perturbation = centred(key_list[1], (TOKENS, PATCH), 0.1, 0.6, ((0, 32),), jnp.float32)
    segment_ids = jax.vmap(lambda own: jnp.searchsorted(jnp.cumsum(uneven(own, SEGS, TOK_ROW, TOK_ROW // 2, 2)), jnp.arange(TOK_ROW), side="right"))(jax.random.split(key_list[2], PACKS)).reshape((PACKS, TOK_ROW)).astype(jnp.int32)
    ball_radius = jnp.clip(jnp.exp(math.log(0.4) - 2.0794415 * jax.random.uniform(key_list[3], (PACKS, SEGS), jnp.float32) ** block_scale(key_list[3], (PACKS, SEGS), ((0, 32),), -0.2, 0.2)), 0.05, 0.4)
    w_embed = centred(key_list[4], (PATCH, D), PATCH ** -0.5, 0.21875)
    gain_attn = jnp.clip(1.0 + 0.1 * jax.random.normal(key_list[5], (D,), jnp.float32), 0.5, 1.5)
    w_qkv = centred(key_list[6], (D, 3, D), D ** -0.5, 0.1875, ((0, 32), (2, 16)))
    w_out = centred(key_list[7], (D, D), D ** -0.5, 0.1875, ((0, 16), (1, 32)))
    gain_mlp = jnp.clip(1.0 + 0.1 * jax.random.normal(key_list[8], (D,), jnp.float32), 0.5, 1.5)
    w_up = centred(key_list[9], (D, FF), D ** -0.5, 0.1875, ((0, 32), (1, 16)))
    w_down = centred(key_list[10], (FF, D), FF ** -0.5, 0.09375, ((0, 16), (1, 32)))
    out_grad = centred(key_list[11], (TOKENS, D), 1.0, 6.0, ((0, 32),))
    return dict(pixels=pixels, perturbation=perturbation, segment_ids=segment_ids, ball_radius=ball_radius, w_embed=w_embed, gain_attn=gain_attn, w_qkv=w_qkv, w_out=w_out, gain_mlp=gain_mlp, w_up=w_up, w_down=w_down, out_grad=out_grad)


STEP_SIZE = 0.1

def layer_norm(values, gain):
    center = lax.optimization_barrier(jnp.mean(values, -1, keepdims=True))
    shifted = values - center
    spread = lax.optimization_barrier(jnp.mean(shifted * shifted, -1, keepdims=True))
    return shifted * lax.rsqrt(spread + 1e-05) * gain

def norm_back(values, gain, upstream):
    _, pull = jax.vjp(lambda t: layer_norm(t, gain), values)
    return pull(upstream)[0]

def gelu_back(values, upstream):
    _, pull = jax.vjp(jax.nn.gelu, values)
    return pull(upstream)[0]

def group_sum(left, right):
    count, inner = left.shape
    part = inner // N_HEADS
    lhs = left.astype(jnp.float32).reshape(count, N_HEADS, part)
    rhs = right.astype(jnp.float32).reshape(N_HEADS, part, right.shape[1])
    terms = jnp.einsum('tgk,gkd->tgd', lhs, rhs).astype(jnp.bfloat16)
    terms = lax.optimization_barrier(terms)
    return lax.optimization_barrier(jnp.sum(terms.astype(jnp.float32), 1))

def group_back(grads, weights):
    count = grads.shape[0]
    width = weights.shape[0]
    part = width // N_HEADS
    lhs = grads.astype(jnp.float32).reshape(count, 3, N_HEADS, part)
    rhs = weights.astype(jnp.float32).reshape(width, 3, N_HEADS, part)
    terms = jnp.einsum('tcgf,dcgf->tgd', lhs, rhs).astype(jnp.bfloat16)
    terms = lax.optimization_barrier(terms)
    return lax.optimization_barrier(jnp.sum(terms.astype(jnp.float32), 1))

def split_heads(projected):
    count, _, width = projected.shape
    size = D // HEADS
    parts = projected.astype(jnp.float32).reshape(count, 3, width // size, size)
    return (parts[:, 0], parts[:, 1], parts[:, 2])

def attend(projected, same):
    count, _, width = projected.shape
    query, keys, values = split_heads(projected)
    scale = 1.0 / math.sqrt(D // HEADS)
    scores = jnp.einsum('qhd,khd->hqk', query, keys) * scale
    powers = jnp.where(same[None], jnp.exp(scores), 0.0)
    shares = powers / lax.optimization_barrier(jnp.sum(powers, -1, keepdims=True))
    shares_low = shares.astype(jnp.bfloat16)
    mixed = jnp.einsum('hqk,khd->qhd', shares_low.astype(jnp.float32), values)
    return (mixed.astype(jnp.bfloat16).reshape(count, width), shares, shares_low)

def attend_back(grad_heads, projected, shares, shares_low):
    count, _, width = projected.shape
    query, keys, values = split_heads(projected)
    size = D // HEADS
    scale = 1.0 / math.sqrt(size)
    upstream = grad_heads.astype(jnp.float32).reshape(count, width // size, size)
    grad_shares = jnp.einsum('qhd,khd->hqk', upstream, values)
    grad_value = jnp.einsum('hqk,qhd->khd', shares_low.astype(jnp.float32), upstream).astype(jnp.bfloat16)
    inner = lax.optimization_barrier(jnp.sum(grad_shares * shares, -1, keepdims=True))
    grad_scores = (shares * (grad_shares - inner) * scale).astype(jnp.bfloat16).astype(jnp.float32)
    grad_query = jnp.einsum('hqk,khd->qhd', grad_scores, keys).astype(jnp.bfloat16)
    grad_key = jnp.einsum('hqk,qhd->khd', grad_scores, query).astype(jnp.bfloat16)
    return jnp.stack([grad_query, grad_key, grad_value], 1).reshape(count, 3, width)

def reference(pixels, perturbation, segment_ids, ball_radius, w_embed, gain_attn, w_qkv, w_out, gain_mlp, w_up, w_down, out_grad):

    def one_pack(items):
        patches, noise, labels, bounds, upstream = items
        same = labels[:, None] == labels[None, :]
        inputs = (patches + noise).astype(jnp.bfloat16)
        embedded = jnp.dot(inputs, w_embed, preferred_element_type=jnp.float32)
        normed_one = layer_norm(embedded, gain_attn).astype(jnp.bfloat16)
        projected = jnp.dot(normed_one, w_qkv.reshape(D, 3 * D), preferred_element_type=jnp.float32)
        projected = projected.reshape(TOK_ROW, 3, D).astype(jnp.bfloat16)
        attended, shares, shares_low = attend(projected, same)
        stream_mid = embedded + group_sum(attended, w_out)
        normed_two = layer_norm(stream_mid, gain_mlp).astype(jnp.bfloat16)
        hidden_pre = jnp.dot(normed_two, w_up, preferred_element_type=jnp.float32)
        hidden_act = jax.nn.gelu(hidden_pre).astype(jnp.bfloat16)
        stream_out = stream_mid + group_sum(hidden_act, w_down)
        grad_hidden = jnp.dot(upstream, w_down.T, preferred_element_type=jnp.float32)
        grad_pre = gelu_back(hidden_pre, grad_hidden).astype(jnp.bfloat16)
        grad_mid = upstream.astype(jnp.float32) + norm_back(stream_mid, gain_mlp, group_sum(grad_pre, w_up.T))
        grad_heads = jnp.dot(grad_mid.astype(jnp.bfloat16), w_out.T, preferred_element_type=jnp.float32).astype(jnp.bfloat16)
        grad_proj = attend_back(grad_heads, projected, shares, shares_low)
        grad_embed = grad_mid + norm_back(embedded, gain_attn, group_back(grad_proj, w_qkv))
        grad_input = jnp.dot(grad_embed.astype(jnp.bfloat16), w_embed.T, preferred_element_type=jnp.float32)
        onehot = (labels[:, None] == jnp.arange(SEGS, dtype=jnp.int32)[None, :]).astype(jnp.float32)
        counts = lax.optimization_barrier(jnp.sum(onehot, 0)) * PATCH
        grad_sq = lax.optimization_barrier(jnp.sum(onehot * lax.optimization_barrier(jnp.sum(grad_input * grad_input, 1))[:, None], 0))
        scale = STEP_SIZE * lax.rsqrt(grad_sq / counts + 1e-06)
        candidate = noise + lax.optimization_barrier(jnp.sum(onehot * scale[None, :], 1))[:, None] * grad_input
        cand_sq = lax.optimization_barrier(jnp.sum(onehot * lax.optimization_barrier(jnp.sum(candidate * candidate, 1))[:, None], 0))
        factor = jnp.minimum(1.0, bounds * lax.rsqrt(cand_sq / counts + 1e-06))
        updated = candidate * lax.optimization_barrier(jnp.sum(onehot * factor[None, :], 1))[:, None]
        return (stream_out.astype(jnp.bfloat16), updated)
    block_out, updated = lax.map(one_pack, (pixels.reshape(N_ROWS, TOK_ROW, PATCH), perturbation.reshape(N_ROWS, TOK_ROW, PATCH), segment_ids, ball_radius, out_grad.reshape(N_ROWS, TOK_ROW, D)))
    return (block_out.reshape(TOKENS, D), updated.reshape(TOKENS, PATCH))
```

```python
import math

import jax
import jax.numpy as jnp
from jax import lax
from jax.experimental import pallas as pl
from jax.experimental.pallas import tpu as pltpu
from jax.sharding import PartitionSpec as P

HEADS = 16
STEP_SIZE = 0.1
VMEM_LIMIT = 56 * 1024 * 1024
F32 = jnp.float32
BF16 = jnp.bfloat16


def mm(a, b):
    return lax.dot_general(a, b, (((1,), (0,)), ((), ())), preferred_element_type=F32)


def mm_nt(a, b):
    return lax.dot_general(a, b, (((1,), (1,)), ((), ())), preferred_element_type=F32)


def mm_tn(a, b):
    return lax.dot_general(a, b, (((0,), (0,)), ((), ())), preferred_element_type=F32)


def normalize(values):
    center = jnp.mean(values, -1, keepdims=True)
    shifted = values - center
    spread = jnp.mean(shifted * shifted, -1, keepdims=True)
    inv = lax.rsqrt(spread + 1e-05)
    return shifted * inv, inv


def norm_back(values, gain, upstream):
    hat, inv = normalize(values)
    scaled = upstream * gain
    return inv * (
        scaled
        - jnp.mean(scaled, -1, keepdims=True)
        - hat * jnp.mean(scaled * hat, -1, keepdims=True)
    )


def head_mask(shape, head, size):
    lane = lax.broadcasted_iota(jnp.int32, shape, 1)
    return (lane >= head * size) & (lane < (head + 1) * size)


def softmax_shares(query, keys, same, scale):
    scores = mm_nt(query, keys) * scale
    powers = jnp.where(same, jnp.exp(scores), 0.0)
    return powers * (1.0 / jnp.sum(powers, -1, keepdims=True))


def attention_kernel(
    size,
    pix_ref, pert_ref, emb_w_ref, gain1_ref, gain2_ref, col_ref, row_ref,
    wq_ref, wk_ref, wv_ref, wo_ref,
    emb_ref, q_ref, k_ref, v_ref, mid_ref, n2_ref,
    n1_ref,
):
    step = pl.program_id(0)

    @pl.when(step == 0)
    def _():
        inputs = (pix_ref[...] + pert_ref[...]).astype(BF16)
        embedded = mm(inputs, emb_w_ref[...])
        emb_ref[...] = embedded
        n1_ref[...] = (normalize(embedded)[0] * gain1_ref[...]).astype(BF16)
        mid_ref[...] = embedded

    n1 = n1_ref[...]
    query = mm(n1, wq_ref[...]).astype(BF16)
    keys = mm(n1, wk_ref[...]).astype(BF16)
    vals = mm(n1, wv_ref[...]).astype(BF16)
    q_ref[...] = query
    k_ref[...] = keys
    v_ref[...] = vals
    same = col_ref[...] == row_ref[...]
    width = query.shape[1]
    scale = 1.0 / math.sqrt(size)
    attended = jnp.zeros(query.shape, F32)
    for head in range(width // size):
        mask = head_mask(query.shape, head, size)
        own = jnp.where(mask, query, jnp.zeros_like(query))
        low = softmax_shares(own, keys, same, scale).astype(BF16)
        attended = jnp.where(mask, mm(low, vals), attended)
    mid_ref[...] += mm_nt(attended.astype(BF16), wo_ref[...])

    @pl.when(step == pl.num_programs(0) - 1)
    def _():
        n2_ref[...] = (normalize(mid_ref[...])[0] * gain2_ref[...]).astype(BF16)


def mlp_kernel(
    n2_ref, og_ref, mid_ref, gain_ref, up_ref, down_ref, out_ref, grad_ref, acc_out, acc_grad
):
    step = pl.program_id(0)

    @pl.when(step == 0)
    def _():
        acc_out[...] = mid_ref[...]
        acc_grad[...] = jnp.zeros_like(acc_grad)

    up = up_ref[...]
    down = down_ref[...]
    pre = mm(n2_ref[...], up)
    grad_hidden = mm(og_ref[...], down)
    root = math.sqrt(2.0 / math.pi)
    square = pre * pre
    tanh = jnp.tanh(root * pre * (1.0 + 0.044715 * square))
    half = 0.5 * (1.0 + tanh)
    act = (pre * half).astype(BF16)
    slope = half + 0.5 * pre * (1.0 - tanh * tanh) * (root * (1.0 + 3.0 * 0.044715 * square))
    grad_pre = (grad_hidden * slope).astype(BF16)
    acc_out[...] += mm_nt(act, down)
    acc_grad[...] += mm_nt(grad_pre, up)

    @pl.when(step == pl.num_programs(0) - 1)
    def _():
        out_ref[...] = acc_out[...].astype(BF16)
        grad_ref[...] = og_ref[...].astype(F32) + norm_back(
            mid_ref[...], gain_ref[...], acc_grad[...]
        )


def backward_kernel(
    size, images,
    grad_ref, emb_ref, gain_ref, emb_w_ref, pert_ref, ball_ref, col_ref, row_ref,
    q_ref, k_ref, v_ref, wq_ref, wk_ref, wv_ref, wo_ref,
    out_ref,
    low_ref, acc_ref,
):
    step = pl.program_id(0)

    @pl.when(step == 0)
    def _():
        low_ref[...] = grad_ref[...].astype(BF16)
        acc_ref[...] = jnp.zeros_like(acc_ref)

    grad_heads = mm(low_ref[...], wo_ref[...]).astype(BF16)
    query, keys, vals = q_ref[...], k_ref[...], v_ref[...]
    same = col_ref[...] == row_ref[...]
    width = query.shape[1]
    scale = 1.0 / math.sqrt(size)
    zero = jnp.zeros_like(query)
    grad_query = jnp.zeros(query.shape, F32)
    grad_keys = jnp.zeros(query.shape, F32)
    grad_vals = jnp.zeros(query.shape, F32)
    for head in range(width // size):
        mask = head_mask(query.shape, head, size)
        shares = softmax_shares(jnp.where(mask, query, zero), keys, same, scale)
        grad_shares = mm_nt(jnp.where(mask, grad_heads, zero), vals)
        grad_vals = jnp.where(mask, mm_tn(shares.astype(BF16), grad_heads), grad_vals)
        inner = jnp.sum(grad_shares * shares, -1, keepdims=True)
        grad_scores = (shares * (grad_shares - inner) * scale).astype(BF16)
        grad_query = jnp.where(mask, mm(grad_scores, keys), grad_query)
        grad_keys = jnp.where(mask, mm_tn(grad_scores, query), grad_keys)
    acc_ref[...] += (
        mm_nt(grad_query.astype(BF16), wq_ref[...])
        + mm_nt(grad_keys.astype(BF16), wk_ref[...])
        + mm_nt(grad_vals.astype(BF16), wv_ref[...])
    )

    @pl.when(step == pl.num_programs(0) - 1)
    def _():
        grad_embed = grad_ref[...] + norm_back(emb_ref[...], gain_ref[...], acc_ref[...])
        grad_input = mm_nt(grad_embed.astype(BF16), emb_w_ref[...])
        labels = col_ref[...]
        noise = pert_ref[...]
        patch = noise.shape[1]
        row_sq = jnp.sum(grad_input * grad_input, -1, keepdims=True)
        scale_rows = jnp.zeros_like(row_sq)
        counts = []
        for image in range(images):
            own = labels == image
            count = jnp.sum(jnp.where(own, 1.0, 0.0), 0, keepdims=True) * patch
            counts.append(count)
            total = jnp.sum(jnp.where(own, row_sq, 0.0), 0, keepdims=True)
            scale_rows = jnp.where(own, STEP_SIZE * lax.rsqrt(total / count + 1e-06), scale_rows)
        candidate = noise + scale_rows * grad_input
        row_sq = jnp.sum(candidate * candidate, -1, keepdims=True)
        factor_rows = jnp.zeros_like(row_sq)
        for image in range(images):
            own = labels == image
            total = jnp.sum(jnp.where(own, row_sq, 0.0), 0, keepdims=True)
            factor = jnp.minimum(
                1.0, ball_ref[:, image : image + 1] * lax.rsqrt(total / counts[image] + 1e-06)
            )
            factor_rows = jnp.where(own, factor, factor_rows)
        out_ref[...] = candidate * factor_rows


def whole(array):
    return pl.BlockSpec(array.shape, lambda j: (0,) * array.ndim)


def params():
    return pltpu.CompilerParams(
        dimension_semantics=("arbitrary",), vmem_limit_bytes=VMEM_LIMIT
    )


def body(
    pixels,
    perturbation,
    segment_ids,
    ball_radius,
    w_embed,
    gain_attn,
    w_qkv,
    w_out,
    gain_mlp,
    w_up,
    w_down,
    out_grad,
):
    rows, patch = pixels.shape
    model = w_embed.shape[1]
    chunk, _, share = w_qkv.shape
    units = w_up.shape[1]
    size = model // HEADS
    groups = model // share
    images = ball_radius.shape[1]

    mine = jnp.concatenate([w_qkv.reshape(chunk, 3 * share), w_out.T, w_up, w_down.T], 1)
    chunks = lax.all_gather(mine, "heads", axis=0, tiled=False)
    attn = chunks[:, :, : 4 * share].reshape(groups, chunk, 4, share)
    attn = attn.transpose(1, 2, 0, 3).reshape(chunk, 4 * model)
    mlp = chunks[:, :, 4 * share :].reshape(groups, chunk, 2, units)
    mlp = mlp.transpose(1, 2, 0, 3).reshape(chunk, 2 * groups * units)
    weights = lax.all_gather(jnp.concatenate([attn, mlp], 1), "rows", axis=0, tiled=True)

    labels_col = segment_ids.reshape(rows, 1)
    labels_row = segment_ids.reshape(1, rows)
    gain1 = gain_attn.reshape(1, model)
    gain2 = gain_mlp.reshape(1, model)

    quad = 4 * size
    steps = model // quad
    full = lambda dt: jax.ShapeDtypeStruct((rows, model), dt)
    block = pl.BlockSpec((rows, quad), lambda j: (0, j))
    fixed = pl.BlockSpec((rows, model), lambda j: (0, 0))
    part = lambda which: pl.BlockSpec((model, quad), lambda j: (0, which * steps + j))

    attn_in = (pixels, perturbation, w_embed, gain1, gain2, labels_col, labels_row)
    embedded, query, keys, vals, stream_mid, normed_two = pl.pallas_call(
        lambda *refs: attention_kernel(size, *refs),
        grid=(steps,),
        in_specs=[whole(a) for a in attn_in] + [part(0), part(1), part(2), part(3)],
        out_specs=[fixed, block, block, block, fixed, fixed],
        out_shape=[full(F32), full(BF16), full(BF16), full(BF16), full(F32), full(BF16)],
        scratch_shapes=[pltpu.VMEM((rows, model), BF16)],
        compiler_params=params(),
    )(*attn_in, weights, weights, weights, weights)

    width = 512
    count = groups * units // width
    first = 4 * model // width
    mlp_in = (normed_two, out_grad, stream_mid, gain2)
    block_out, grad_mid = pl.pallas_call(
        mlp_kernel,
        grid=(count,),
        in_specs=[whole(a) for a in mlp_in]
        + [
            pl.BlockSpec((model, width), lambda j: (0, first + j)),
            pl.BlockSpec((model, width), lambda j: (0, first + count + j)),
        ],
        out_specs=[fixed, fixed],
        out_shape=[full(BF16), full(F32)],
        scratch_shapes=[pltpu.VMEM((rows, model), F32), pltpu.VMEM((rows, model), F32)],
        compiler_params=params(),
    )(*mlp_in, weights, weights)

    back_in = (grad_mid, embedded, gain1, w_embed, perturbation, ball_radius, labels_col, labels_row)
    updated = pl.pallas_call(
        lambda *refs: backward_kernel(size, images, *refs),
        grid=(steps,),
        in_specs=[whole(a) for a in back_in]
        + [block, block, block, part(0), part(1), part(2), part(3)],
        out_specs=pl.BlockSpec((rows, patch), lambda j: (0, 0)),
        out_shape=jax.ShapeDtypeStruct((rows, patch), F32),
        scratch_shapes=[pltpu.VMEM((rows, model), BF16), pltpu.VMEM((rows, model), F32)],
        compiler_params=params(),
    )(*back_in, query, keys, vals, weights, weights, weights, weights)
    return (block_out, updated)


def solution(mesh):
    in_specs = (
        P("rows", None),
        P("rows", None),
        P("rows", None),
        P("rows", None),
        P(),
        P(),
        P("rows", None, "heads"),
        P("heads", "rows"),
        P(),
        P("rows", "heads"),
        P("heads", "rows"),
        P("rows", None),
    )
    out_specs = (P("rows", None), P("rows", None))
    return jax.shard_map(body, mesh=mesh, in_specs=in_specs, out_specs=out_specs, check_vma=False)
```

```python
import math

import jax
import jax.numpy as jnp
from jax import lax
from jax.experimental import pallas as pl
from jax.experimental.pallas import tpu as pltpu
from jax.sharding import PartitionSpec as P

HEADS = 16
STEP_SIZE = 0.1
VMEM_LIMIT = 56 * 1024 * 1024
F32 = jnp.float32
BF16 = jnp.bfloat16


def mm(a, b):
    return lax.dot_general(a, b, (((1,), (0,)), ((), ())), preferred_element_type=F32)


def mm_nt(a, b):
    return lax.dot_general(a, b, (((1,), (1,)), ((), ())), preferred_element_type=F32)


def mm_tn(a, b):
    return lax.dot_general(a, b, (((0,), (0,)), ((), ())), preferred_element_type=F32)


def normalize(values):
    center = jnp.mean(values, -1, keepdims=True)
    shifted = values - center
    spread = jnp.mean(shifted * shifted, -1, keepdims=True)
    inv = lax.rsqrt(spread + 1e-05)
    return shifted * inv, inv


def norm_back(values, gain, upstream):
    hat, inv = normalize(values)
    scaled = upstream * gain
    return inv * (
        scaled
        - jnp.mean(scaled, -1, keepdims=True)
        - hat * jnp.mean(scaled * hat, -1, keepdims=True)
    )


def reorder(values, perm):
    high = values.astype(BF16)
    rest = (values - high.astype(F32)).astype(BF16)
    return mm_nt(high, perm) + mm_nt(rest, perm)


def head_mask(shape, head, size):
    lane = lax.broadcasted_iota(jnp.int32, shape, 1)
    return (lane >= head * size) & (lane < (head + 1) * size)


def softmax_shares(query, keys, same, scale):
    scores = mm_nt(query, keys) * scale
    powers = jnp.where(same, jnp.exp(scores), 0.0)
    return powers * (1.0 / jnp.sum(powers, -1, keepdims=True))


def attention_kernel(
    size,
    pix_ref, pert_ref, emb_w_ref, gain1_ref, gain2_ref, col_ref, row_ref, perm_ref,
    wq0_ref, wq1_ref, wk0_ref, wk1_ref, wv0_ref, wv1_ref, wo0_ref, wo1_ref,
    emb_ref, q_ref, k_ref, v_ref, mid_ref, n2_ref,
    n1_ref, acc_ref,
):
    step = pl.program_id(0)

    @pl.when(step == 0)
    def _():
        inputs = (pix_ref[...] + pert_ref[...]).astype(BF16)
        embedded = mm(inputs, emb_w_ref[...])
        emb_ref[...] = embedded
        normed = (normalize(embedded)[0] * gain1_ref[...]).astype(BF16)
        n1_ref[...] = mm(normed, perm_ref[...]).astype(BF16)
        acc_ref[...] = jnp.zeros_like(acc_ref)

    half = n1_ref.shape[1] // 2
    own, other = n1_ref[:, :half], n1_ref[:, half:]
    query = (mm(own, wq0_ref[...]) + mm(other, wq1_ref[...])).astype(BF16)
    keys = (mm(own, wk0_ref[...]) + mm(other, wk1_ref[...])).astype(BF16)
    vals = (mm(own, wv0_ref[...]) + mm(other, wv1_ref[...])).astype(BF16)
    q_ref[...] = query
    k_ref[...] = keys
    v_ref[...] = vals
    same = col_ref[...] == row_ref[...]
    width = query.shape[1]
    scale = 1.0 / math.sqrt(size)
    attended = jnp.zeros(query.shape, F32)
    for head in range(width // size):
        mask = head_mask(query.shape, head, size)
        masked = jnp.where(mask, query, jnp.zeros_like(query))
        low = softmax_shares(masked, keys, same, scale).astype(BF16)
        attended = jnp.where(mask, mm(low, vals), attended)
    attended = attended.astype(BF16)
    acc_ref[:, :half] += mm_nt(attended, wo0_ref[...])
    acc_ref[:, half:] += mm_nt(attended, wo1_ref[...])

    @pl.when(step == pl.num_programs(0) - 1)
    def _():
        mid_ref[...] = emb_ref[...] + reorder(acc_ref[...], perm_ref[...])
        n2_ref[...] = (normalize(mid_ref[...])[0] * gain2_ref[...]).astype(BF16)


def mlp_kernel(
    n2_ref, og_ref, mid_ref, gain_ref, up_ref, down_ref, out_ref, grad_ref, acc_out, acc_grad
):
    step = pl.program_id(0)

    @pl.when(step == 0)
    def _():
        acc_out[...] = mid_ref[...]
        acc_grad[...] = jnp.zeros_like(acc_grad)

    up = up_ref[...]
    down = down_ref[...]
    pre = mm(n2_ref[...], up)
    grad_hidden = mm(og_ref[...], down)
    root = math.sqrt(2.0 / math.pi)
    square = pre * pre
    tanh = jnp.tanh(root * pre * (1.0 + 0.044715 * square))
    half = 0.5 * (1.0 + tanh)
    act = (pre * half).astype(BF16)
    slope = half + 0.5 * pre * (1.0 - tanh * tanh) * (root * (1.0 + 3.0 * 0.044715 * square))
    grad_pre = (grad_hidden * slope).astype(BF16)
    acc_out[...] += mm_nt(act, down)
    acc_grad[...] += mm_nt(grad_pre, up)

    @pl.when(step == pl.num_programs(0) - 1)
    def _():
        out_ref[...] = acc_out[...].astype(BF16)
        grad_ref[...] = og_ref[...].astype(F32) + norm_back(
            mid_ref[...], gain_ref[...], acc_grad[...]
        )


def backward_kernel(
    size, images,
    grad_ref, emb_ref, gain_ref, emb_w_ref, pert_ref, ball_ref, col_ref, row_ref, perm_ref,
    q_ref, k_ref, v_ref,
    wq0_ref, wq1_ref, wk0_ref, wk1_ref, wv0_ref, wv1_ref, wo0_ref, wo1_ref,
    out_ref,
    low_ref, acc_ref,
):
    step = pl.program_id(0)

    @pl.when(step == 0)
    def _():
        low_ref[...] = mm(grad_ref[...].astype(BF16), perm_ref[...]).astype(BF16)
        acc_ref[...] = jnp.zeros_like(acc_ref)

    half = low_ref.shape[1] // 2
    grad_heads = mm(low_ref[:, :half], wo0_ref[...]) + mm(low_ref[:, half:], wo1_ref[...])
    grad_heads = grad_heads.astype(BF16)
    query, keys, vals = q_ref[...], k_ref[...], v_ref[...]
    same = col_ref[...] == row_ref[...]
    width = query.shape[1]
    scale = 1.0 / math.sqrt(size)
    zero = jnp.zeros_like(query)
    grad_query = jnp.zeros(query.shape, F32)
    grad_keys = jnp.zeros(query.shape, F32)
    grad_vals = jnp.zeros(query.shape, F32)
    for head in range(width // size):
        mask = head_mask(query.shape, head, size)
        shares = softmax_shares(jnp.where(mask, query, zero), keys, same, scale)
        grad_shares = mm_nt(jnp.where(mask, grad_heads, zero), vals)
        grad_vals = jnp.where(mask, mm_tn(shares.astype(BF16), grad_heads), grad_vals)
        inner = jnp.sum(grad_shares * shares, -1, keepdims=True)
        grad_scores = (shares * (grad_shares - inner) * scale).astype(BF16)
        grad_query = jnp.where(mask, mm(grad_scores, keys), grad_query)
        grad_keys = jnp.where(mask, mm_tn(grad_scores, query), grad_keys)
    grad_query, grad_keys = grad_query.astype(BF16), grad_keys.astype(BF16)
    grad_vals = grad_vals.astype(BF16)
    acc_ref[:, :half] += (
        mm_nt(grad_query, wq0_ref[...])
        + mm_nt(grad_keys, wk0_ref[...])
        + mm_nt(grad_vals, wv0_ref[...])
    )
    acc_ref[:, half:] += (
        mm_nt(grad_query, wq1_ref[...])
        + mm_nt(grad_keys, wk1_ref[...])
        + mm_nt(grad_vals, wv1_ref[...])
    )

    @pl.when(step == pl.num_programs(0) - 1)
    def _():
        grad_norm = reorder(acc_ref[...], perm_ref[...])
        grad_embed = grad_ref[...] + norm_back(emb_ref[...], gain_ref[...], grad_norm)
        grad_input = mm_nt(grad_embed.astype(BF16), emb_w_ref[...])
        labels = col_ref[...]
        noise = pert_ref[...]
        patch = noise.shape[1]
        row_sq = jnp.sum(grad_input * grad_input, -1, keepdims=True)
        scale_rows = jnp.zeros_like(row_sq)
        counts = []
        for image in range(images):
            own = labels == image
            count = jnp.sum(jnp.where(own, 1.0, 0.0), 0, keepdims=True) * patch
            counts.append(count)
            total = jnp.sum(jnp.where(own, row_sq, 0.0), 0, keepdims=True)
            scale_rows = jnp.where(own, STEP_SIZE * lax.rsqrt(total / count + 1e-06), scale_rows)
        candidate = noise + scale_rows * grad_input
        row_sq = jnp.sum(candidate * candidate, -1, keepdims=True)
        factor_rows = jnp.zeros_like(row_sq)
        for image in range(images):
            own = labels == image
            total = jnp.sum(jnp.where(own, row_sq, 0.0), 0, keepdims=True)
            factor = jnp.minimum(
                1.0, ball_ref[:, image : image + 1] * lax.rsqrt(total / counts[image] + 1e-06)
            )
            factor_rows = jnp.where(own, factor, factor_rows)
        out_ref[...] = candidate * factor_rows


def whole(array):
    return pl.BlockSpec(array.shape, lambda j: (0,) * array.ndim)


def params():
    return pltpu.CompilerParams(
        dimension_semantics=("arbitrary",), vmem_limit_bytes=VMEM_LIMIT
    )


def body(
    pixels,
    perturbation,
    segment_ids,
    ball_radius,
    w_embed,
    gain_attn,
    w_qkv,
    w_out,
    gain_mlp,
    w_up,
    w_down,
    out_grad,
):
    rows, patch = pixels.shape
    model = w_embed.shape[1]
    chunk, _, share = w_qkv.shape
    units = w_up.shape[1]
    size = model // HEADS
    groups = model // share
    images = ball_radius.shape[1]

    mine = jnp.concatenate([w_qkv.reshape(chunk, 3 * share), w_out.T, w_up, w_down.T], 1)
    chunks = lax.all_gather(mine, "heads", axis=0, tiled=False)
    attn = chunks[:, :, : 4 * share].reshape(groups, chunk, 4, share)
    attn = attn.transpose(1, 2, 0, 3).reshape(chunk, 4 * model)
    mlp = chunks[:, :, 4 * share :].reshape(groups, chunk, 2, units)
    mlp = mlp.transpose(1, 2, 0, 3).reshape(chunk, 2 * groups * units)
    weights = lax.all_gather(mlp, "rows", axis=0, tiled=True)

    sites = lax.axis_size("rows") // 2
    planes = [[2 * site + core for site in range(sites)] for core in range(2)]
    copies = jnp.broadcast_to(attn[None], (sites,) + attn.shape)
    near = lax.all_to_all(copies, "rows", 0, 0, axis_index_groups=planes)
    near = near.reshape(sites * chunk, 4 * model)
    far = lax.ppermute(near, "rows", [(row, row ^ 1) for row in range(2 * sites)])

    core = lax.axis_index("rows") % 2
    place = jnp.arange(model)
    source = jnp.where(place < model // 2, core, 1 - core) + 2 * (place % (model // 2) // chunk)
    source = source * chunk + place % chunk
    perm = (place[:, None] == source[None, :]).astype(BF16)

    labels_col = segment_ids.reshape(rows, 1)
    labels_row = segment_ids.reshape(1, rows)
    gain1 = gain_attn.reshape(1, model)
    gain2 = gain_mlp.reshape(1, model)

    quad = 4 * size
    steps = model // quad
    full = lambda dt: jax.ShapeDtypeStruct((rows, model), dt)
    block = pl.BlockSpec((rows, quad), lambda j: (0, j))
    fixed = pl.BlockSpec((rows, model), lambda j: (0, 0))
    part = lambda which: pl.BlockSpec((model // 2, quad), lambda j: (0, which * steps + j))
    parts = [part(which) for which in range(4) for _ in range(2)]

    attn_in = (pixels, perturbation, w_embed, gain1, gain2, labels_col, labels_row, perm)
    embedded, query, keys, vals, stream_mid, normed_two = pl.pallas_call(
        lambda *refs: attention_kernel(size, *refs),
        grid=(steps,),
        in_specs=[whole(a) for a in attn_in] + parts,
        out_specs=[fixed, block, block, block, fixed, fixed],
        out_shape=[full(F32), full(BF16), full(BF16), full(BF16), full(F32), full(BF16)],
        scratch_shapes=[pltpu.VMEM((rows, model), BF16), pltpu.VMEM((rows, model), F32)],
        compiler_params=params(),
    )(*attn_in, *[near, far] * 4)

    width = 512
    count = groups * units // width
    mlp_in = (normed_two, out_grad, stream_mid, gain2)
    block_out, grad_mid = pl.pallas_call(
        mlp_kernel,
        grid=(count,),
        in_specs=[whole(a) for a in mlp_in]
        + [
            pl.BlockSpec((model, width), lambda j: (0, j)),
            pl.BlockSpec((model, width), lambda j: (0, count + j)),
        ],
        out_specs=[fixed, fixed],
        out_shape=[full(BF16), full(F32)],
        scratch_shapes=[pltpu.VMEM((rows, model), F32), pltpu.VMEM((rows, model), F32)],
        compiler_params=params(),
    )(*mlp_in, weights, weights)

    back_in = (grad_mid, embedded, gain1, w_embed, perturbation, ball_radius)
    back_in = back_in + (labels_col, labels_row, perm)
    updated = pl.pallas_call(
        lambda *refs: backward_kernel(size, images, *refs),
        grid=(steps,),
        in_specs=[whole(a) for a in back_in]
        + [block, block, block]
        + parts,
        out_specs=pl.BlockSpec((rows, patch), lambda j: (0, 0)),
        out_shape=jax.ShapeDtypeStruct((rows, patch), F32),
        scratch_shapes=[pltpu.VMEM((rows, model), BF16), pltpu.VMEM((rows, model), F32)],
        compiler_params=params(),
    )(*back_in, query, keys, vals, *[near, far] * 4)
    return (block_out, updated)


def solution(mesh):
    in_specs = (
        P("rows", None),
        P("rows", None),
        P("rows", None),
        P("rows", None),
        P(),
        P(),
        P("rows", None, "heads"),
        P("heads", "rows"),
        P(),
        P("rows", "heads"),
        P("heads", "rows"),
        P("rows", None),
    )
    out_specs = (P("rows", None), P("rows", None))
    return jax.shard_map(body, mesh=mesh, in_specs=in_specs, out_specs=out_specs, check_vma=False)
```

```python
import math

import jax
import jax.numpy as jnp
from jax import lax
from jax.experimental import pallas as pl
from jax.experimental.pallas import tpu as pltpu
from jax.sharding import PartitionSpec as P

HEADS = 16
STEP_SIZE = 0.1
VMEM_LIMIT = 56 * 1024 * 1024
F32 = jnp.float32
BF16 = jnp.bfloat16


def mm(a, b):
    return lax.dot_general(a, b, (((1,), (0,)), ((), ())), preferred_element_type=F32)


def mm_nt(a, b):
    return lax.dot_general(a, b, (((1,), (1,)), ((), ())), preferred_element_type=F32)


def mm_tn(a, b):
    return lax.dot_general(a, b, (((0,), (0,)), ((), ())), preferred_element_type=F32)


def normalize(values):
    center = jnp.mean(values, -1, keepdims=True)
    shifted = values - center
    spread = jnp.mean(shifted * shifted, -1, keepdims=True)
    inv = lax.rsqrt(spread + 1e-05)
    return shifted * inv, inv


def norm_back(values, gain, upstream):
    hat, inv = normalize(values)
    scaled = upstream * gain
    return inv * (
        scaled
        - jnp.mean(scaled, -1, keepdims=True)
        - hat * jnp.mean(scaled * hat, -1, keepdims=True)
    )


def reorder(values, perm):
    high = values.astype(BF16)
    rest = (values - high.astype(F32)).astype(BF16)
    return mm_nt(high, perm) + mm_nt(rest, perm)


def head_mask(shape, head, size):
    lane = lax.broadcasted_iota(jnp.int32, shape, 1)
    return (lane >= head * size) & (lane < (head + 1) * size)


def softmax_shares(query, keys, same, scale):
    scores = mm_nt(query, keys) * scale
    powers = jnp.where(same, jnp.exp(scores), 0.0)
    return powers * (1.0 / jnp.sum(powers, -1, keepdims=True))


def attention_kernel(
    size,
    pix_ref, pert_ref, emb_w_ref, gain1_ref, gain2_ref, col_ref, row_ref, perm_ref,
    wq0_ref, wq1_ref, wk0_ref, wk1_ref, wv0_ref, wv1_ref, wo0_ref, wo1_ref,
    emb_ref, q_ref, k_ref, v_ref, mid_ref, n2_ref, low_ref, turned_ref,
    n1_ref, acc_ref,
):
    step = pl.program_id(0)

    @pl.when(step == 0)
    def _():
        inputs = (pix_ref[...] + pert_ref[...]).astype(BF16)
        embedded = mm(inputs, emb_w_ref[...])
        emb_ref[...] = embedded
        normed = (normalize(embedded)[0] * gain1_ref[...]).astype(BF16)
        n1_ref[...] = mm(normed, perm_ref[...]).astype(BF16)
        acc_ref[...] = jnp.zeros_like(acc_ref)

    half = n1_ref.shape[1] // 2
    own, other = n1_ref[:, :half], n1_ref[:, half:]
    query = (mm(own, wq0_ref[...]) + mm(other, wq1_ref[...])).astype(BF16)
    keys = (mm(own, wk0_ref[...]) + mm(other, wk1_ref[...])).astype(BF16)
    vals = (mm(own, wv0_ref[...]) + mm(other, wv1_ref[...])).astype(BF16)
    q_ref[...] = query
    k_ref[...] = keys
    v_ref[...] = vals
    same = col_ref[...] == row_ref[...]
    width = query.shape[1]
    scale = 1.0 / math.sqrt(size)
    attended = jnp.zeros(query.shape, F32)
    for head in range(width // size):
        mask = head_mask(query.shape, head, size)
        masked = jnp.where(mask, query, jnp.zeros_like(query))
        shares = softmax_shares(masked, keys, same, scale)
        low = shares.astype(BF16)
        low_ref[head] = low
        turned_ref[head] = shares.T.astype(BF16)
        attended = jnp.where(mask, mm(low, vals), attended)
    attended = attended.astype(BF16)
    acc_ref[:, :half] += mm_nt(attended, wo0_ref[...])
    acc_ref[:, half:] += mm_nt(attended, wo1_ref[...])

    @pl.when(step == pl.num_programs(0) - 1)
    def _():
        mid_ref[...] = emb_ref[...] + reorder(acc_ref[...], perm_ref[...])
        n2_ref[...] = (normalize(mid_ref[...])[0] * gain2_ref[...]).astype(BF16)


def tail_kernel(
    size, images,
    n2_hbm, og_hbm, mid_hbm, weights_hbm, near_hbm, far_hbm, q_hbm, k_hbm, v_hbm,
    low_hbm, turned_hbm, emb_hbm, emb_w_hbm, pert_hbm,
    gain1_ref, gain2_ref, ball_ref, col_ref,
    out_ref, new_ref,
    n2_ref, og_ref, mid_ref, up_buf, down_buf, attn_buf, qkv_buf,
    low_buf, turned_buf, emb_ref, emb_w_ref, pert_ref,
    acc_out, acc_grad, heads_ref, proj_ref,
    up_sem, down_sem, sem,
):
    rows, model = n2_ref.shape
    chunks, _, width = up_buf.shape
    core = lax.rem(lax.axis_index("rows"), 2)

    def up_copy(j):
        start = pl.multiple_of(j * width, width)
        source = weights_hbm.at[:, pl.ds(start, width)]
        return pltpu.make_async_copy(source, up_buf.at[j], up_sem.at[j])

    def down_copy(j):
        start = pl.multiple_of((chunks + j) * width, width)
        source = weights_hbm.at[:, pl.ds(start, width)]
        return pltpu.make_async_copy(source, down_buf.at[j], down_sem.at[j])

    pairs = (
        (n2_hbm, n2_ref),
        (og_hbm, og_ref),
        (mid_hbm, mid_ref),
        (near_hbm, attn_buf.at[:, core]),
        (far_hbm, attn_buf.at[:, 1 - core]),
        (q_hbm, qkv_buf.at[0]),
        (k_hbm, qkv_buf.at[1]),
        (v_hbm, qkv_buf.at[2]),
        (low_hbm, low_buf),
        (turned_hbm, turned_buf),
        (emb_hbm, emb_ref),
        (emb_w_hbm, emb_w_ref),
        (pert_hbm, pert_ref),
    )
    copies = [pltpu.make_async_copy(*pair, sem.at[i]) for i, pair in enumerate(pairs)]

    copies[0].start()
    up_copy(0).start()
    copies[1].start()
    down_copy(0).start()
    copies[2].start()
    up_copy(1).start()
    down_copy(1).start()
    acc_out[...] = jnp.zeros_like(acc_out)
    acc_grad[...] = jnp.zeros_like(acc_grad)
    for copy in copies[:2]:
        copy.wait()

    def mlp_step(j, carry):
        @pl.when(j + 2 < chunks)
        def _():
            up_copy(j + 2).start()
            down_copy(j + 2).start()

        @pl.when(j + 2 == chunks)
        def _():
            for copy in copies[3:]:
                copy.start()

        up_copy(j).wait()
        pre = mm(n2_ref[...], up_buf[j])
        down_copy(j).wait()
        grad_hidden = mm(og_ref[...], down_buf[j])
        root = math.sqrt(2.0 / math.pi)
        square = pre * pre
        tanh = jnp.tanh(root * pre * (1.0 + 0.044715 * square))
        half = 0.5 * (1.0 + tanh)
        act = (pre * half).astype(BF16)
        slope = half + 0.5 * pre * (1.0 - tanh * tanh) * (root * (1.0 + 3.0 * 0.044715 * square))
        grad_pre = (grad_hidden * slope).astype(BF16)
        acc_out[...] += mm_nt(act, down_buf[j])
        acc_grad[...] += mm_nt(grad_pre, up_buf[j])
        return carry

    lax.fori_loop(0, chunks, mlp_step, 0)
    copies[2].wait()
    out_ref[...] = (mid_ref[...] + acc_out[...]).astype(BF16)
    grad_mid = og_ref[...].astype(F32) + norm_back(mid_ref[...], gain2_ref[...], acc_grad[...])
    acc_grad[...] = grad_mid
    for copy in copies[3:]:
        copy.wait()

    def weights(first, last):
        return attn_buf[:, :, :, first * model : last * model].reshape(
            model, (last - first) * model
        )

    heads_ref[...] = mm(grad_mid.astype(BF16), weights(3, 4)).astype(BF16)
    quad = 4 * size
    scale = 1.0 / math.sqrt(size)

    def attention_step(j, carry):
        lanes = pl.ds(pl.multiple_of(j * quad, quad), quad)
        query, keys, vals = qkv_buf[0, :, lanes], qkv_buf[1, :, lanes], qkv_buf[2, :, lanes]
        grad_heads = heads_ref[:, lanes]
        zero = jnp.zeros_like(grad_heads)
        grad_query = jnp.zeros((rows, quad), F32)
        grad_keys = jnp.zeros((rows, quad), F32)
        grad_vals = jnp.zeros((rows, quad), F32)
        for head in range(4):
            mask = head_mask((rows, quad), head, size)
            shares = low_buf[j * 4 + head].astype(F32)
            grad_shares = mm_nt(jnp.where(mask, grad_heads, zero), vals)
            grad_vals = jnp.where(mask, mm(turned_buf[j * 4 + head], grad_heads), grad_vals)
            inner = jnp.sum(grad_shares * shares, -1, keepdims=True)
            grad_scores = (shares * (grad_shares - inner) * scale).astype(BF16)
            grad_query = jnp.where(mask, mm(grad_scores, keys), grad_query)
            grad_keys = jnp.where(mask, mm_tn(grad_scores, query), grad_keys)
        for which, value in enumerate((grad_query, grad_keys, grad_vals)):
            start = pl.multiple_of(which * model + j * quad, quad)
            proj_ref[:, pl.ds(start, quad)] = value.astype(BF16)
        return carry

    lax.fori_loop(0, model // quad, attention_step, 0)
    grad_norm = mm_nt(proj_ref[...], weights(0, 3))
    grad_embed = acc_grad[...] + norm_back(emb_ref[...], gain1_ref[...], grad_norm)
    grad_input = mm_nt(grad_embed.astype(BF16), emb_w_ref[...])
    labels = col_ref[...]
    noise = pert_ref[...]
    patch = noise.shape[1]
    row_sq = jnp.sum(grad_input * grad_input, -1, keepdims=True)
    scale_rows = jnp.zeros_like(row_sq)
    counts = []
    for image in range(images):
        own = labels == image
        count = jnp.sum(jnp.where(own, 1.0, 0.0), 0, keepdims=True) * patch
        counts.append(count)
        total = jnp.sum(jnp.where(own, row_sq, 0.0), 0, keepdims=True)
        scale_rows = jnp.where(own, STEP_SIZE * lax.rsqrt(total / count + 1e-06), scale_rows)
    candidate = noise + scale_rows * grad_input
    row_sq = jnp.sum(candidate * candidate, -1, keepdims=True)
    factor_rows = jnp.zeros_like(row_sq)
    for image in range(images):
        own = labels == image
        total = jnp.sum(jnp.where(own, row_sq, 0.0), 0, keepdims=True)
        factor = jnp.minimum(
            1.0, ball_ref[:, image : image + 1] * lax.rsqrt(total / counts[image] + 1e-06)
        )
        factor_rows = jnp.where(own, factor, factor_rows)
    new_ref[...] = candidate * factor_rows


def whole(array):
    return pl.BlockSpec(array.shape, lambda j: (0,) * array.ndim)


def params():
    return pltpu.CompilerParams(
        dimension_semantics=("arbitrary",), vmem_limit_bytes=VMEM_LIMIT
    )


def body(
    pixels,
    perturbation,
    segment_ids,
    ball_radius,
    w_embed,
    gain_attn,
    w_qkv,
    w_out,
    gain_mlp,
    w_up,
    w_down,
    out_grad,
):
    rows, patch = pixels.shape
    model = w_embed.shape[1]
    chunk, _, share = w_qkv.shape
    units = w_up.shape[1]
    size = model // HEADS
    groups = model // share
    images = ball_radius.shape[1]

    mine = jnp.concatenate([w_qkv.reshape(chunk, 3 * share), w_out.T, w_up, w_down.T], 1)
    chunks = lax.all_gather(mine, "heads", axis=0, tiled=False)
    attn = chunks[:, :, : 4 * share].reshape(groups, chunk, 4, share)
    attn = attn.transpose(1, 2, 0, 3).reshape(chunk, 4 * model)
    mlp = chunks[:, :, 4 * share :].reshape(groups, chunk, 2, units)
    mlp = mlp.transpose(1, 2, 0, 3).reshape(chunk, 2 * groups * units)
    weights = lax.all_gather(mlp, "rows", axis=0, tiled=True)

    sites = lax.axis_size("rows") // 2
    planes = [[2 * site + core for site in range(sites)] for core in range(2)]
    copies = jnp.broadcast_to(attn[None], (sites,) + attn.shape)
    near = lax.all_to_all(copies, "rows", 0, 0, axis_index_groups=planes)
    near = near.reshape(sites * chunk, 4 * model)
    far = lax.ppermute(near, "rows", [(row, row ^ 1) for row in range(2 * sites)])

    core = lax.axis_index("rows") % 2
    place = jnp.arange(model)
    source = jnp.where(place < model // 2, core, 1 - core) + 2 * (place % (model // 2) // chunk)
    source = source * chunk + place % chunk
    perm = (place[:, None] == source[None, :]).astype(BF16)

    labels_col = segment_ids.reshape(rows, 1)
    labels_row = segment_ids.reshape(1, rows)
    gain1 = gain_attn.reshape(1, model)
    gain2 = gain_mlp.reshape(1, model)

    quad = 4 * size
    steps = model // quad
    full = lambda dt: jax.ShapeDtypeStruct((rows, model), dt)
    block = pl.BlockSpec((rows, quad), lambda j: (0, j))
    square = pl.BlockSpec((4, rows, rows), lambda j: (j, 0, 0))
    fixed = pl.BlockSpec((rows, model), lambda j: (0, 0))
    part = lambda which: pl.BlockSpec((model // 2, quad), lambda j: (0, which * steps + j))
    parts = [part(which) for which in range(4) for _ in range(2)]

    attn_in = (pixels, perturbation, w_embed, gain1, gain2, labels_col, labels_row, perm)
    embedded, query, keys, vals, stream_mid, normed_two, low, turned = pl.pallas_call(
        lambda *refs: attention_kernel(size, *refs),
        grid=(steps,),
        in_specs=[whole(a) for a in attn_in] + parts,
        out_specs=[fixed, block, block, block, fixed, fixed, square, square],
        out_shape=[full(F32), full(BF16), full(BF16), full(BF16), full(F32), full(BF16)]
        + [jax.ShapeDtypeStruct((HEADS, rows, rows), BF16)] * 2,
        scratch_shapes=[pltpu.VMEM((rows, model), BF16), pltpu.VMEM((rows, model), F32)],
        compiler_params=params(),
    )(*attn_in, *[near, far] * 4)

    width = 1024
    count = groups * units // width
    shard = (sites, chunk, 4 * model)
    moved = (normed_two, out_grad, stream_mid, weights, near.reshape(shard), far.reshape(shard))
    moved = moved + (query, keys, vals, low, turned, embedded, w_embed, perturbation)
    kept = (gain1, gain2, ball_radius, labels_col)
    vmem = pl.BlockSpec(memory_space=pltpu.VMEM)
    block_out, updated = pl.pallas_call(
        lambda *refs: tail_kernel(size, images, *refs),
        in_specs=[pl.BlockSpec(memory_space=pl.ANY)] * len(moved) + [vmem] * len(kept),
        out_specs=[vmem, vmem],
        out_shape=[full(BF16), jax.ShapeDtypeStruct((rows, patch), F32)],
        scratch_shapes=[
            pltpu.VMEM((rows, model), BF16),
            pltpu.VMEM((rows, model), BF16),
            pltpu.VMEM((rows, model), F32),
            pltpu.VMEM((count, model, width), BF16),
            pltpu.VMEM((count, model, width), BF16),
            pltpu.VMEM((sites, 2, chunk, 4 * model), BF16),
            pltpu.VMEM((3, rows, model), BF16),
            pltpu.VMEM((HEADS, rows, rows), BF16),
            pltpu.VMEM((HEADS, rows, rows), BF16),
            pltpu.VMEM((rows, model), F32),
            pltpu.VMEM((patch, model), BF16),
            pltpu.VMEM((rows, patch), F32),
            pltpu.VMEM((rows, model), F32),
            pltpu.VMEM((rows, model), F32),
            pltpu.VMEM((rows, model), BF16),
            pltpu.VMEM((rows, 3 * model), BF16),
            pltpu.SemaphoreType.DMA((count,)),
            pltpu.SemaphoreType.DMA((count,)),
            pltpu.SemaphoreType.DMA((13,)),
        ],
        compiler_params=pltpu.CompilerParams(vmem_limit_bytes=VMEM_LIMIT),
    )(*moved, *kept)
    return (block_out, updated)


def solution(mesh):
    in_specs = (
        P("rows", None),
        P("rows", None),
        P("rows", None),
        P("rows", None),
        P(),
        P(),
        P("rows", None, "heads"),
        P("heads", "rows"),
        P(),
        P("rows", "heads"),
        P("heads", "rows"),
        P("rows", None),
    )
    out_specs = (P("rows", None), P("rows", None))
    return jax.shard_map(body, mesh=mesh, in_specs=in_specs, out_specs=out_specs, check_vma=False)
```

```python
import math

import jax
import jax.numpy as jnp
from jax import lax
from jax.experimental import pallas as pl
from jax.experimental.pallas import tpu as pltpu
from jax.sharding import PartitionSpec as P

HEADS = 16
STEP_SIZE = 0.1
VMEM_LIMIT = 56 * 1024 * 1024
F32 = jnp.float32
BF16 = jnp.bfloat16


def mm(a, b):
    return lax.dot_general(a, b, (((1,), (0,)), ((), ())), preferred_element_type=F32)


def mm_nt(a, b):
    return lax.dot_general(a, b, (((1,), (1,)), ((), ())), preferred_element_type=F32)


def mm_tn(a, b):
    return lax.dot_general(a, b, (((0,), (0,)), ((), ())), preferred_element_type=F32)


def normalize(values):
    center = jnp.mean(values, -1, keepdims=True)
    shifted = values - center
    spread = jnp.mean(shifted * shifted, -1, keepdims=True)
    inv = lax.rsqrt(spread + 1e-05)
    return shifted * inv, inv


def norm_back(values, gain, upstream):
    hat, inv = normalize(values)
    scaled = upstream * gain
    return inv * (
        scaled
        - jnp.mean(scaled, -1, keepdims=True)
        - hat * jnp.mean(scaled * hat, -1, keepdims=True)
    )


def head_mask(shape, head, size):
    lane = lax.broadcasted_iota(jnp.int32, shape, 1)
    return (lane >= head * size) & (lane < (head + 1) * size)


def softmax_shares(query, keys, same, scale):
    scores = mm_nt(query, keys) * scale
    powers = jnp.where(same, jnp.exp(scores), 0.0)
    return powers * (1.0 / jnp.sum(powers, -1, keepdims=True))


def embed_kernel(pix_ref, pert_ref, weight_ref, gain_ref, emb_ref, n1_ref):
    inputs = (pix_ref[...] + pert_ref[...]).astype(BF16)
    embedded = mm(inputs, weight_ref[...])
    emb_ref[...] = embedded
    n1_ref[...] = (normalize(embedded)[0] * gain_ref[...]).astype(BF16)


def columns(buf, first, last):
    sites, cores, chunk, width = buf.shape
    model = sites * cores * chunk
    return buf[:, :, :, first * model : last * model].reshape(model, (last - first) * model)


def attention_kernel(
    size,
    n1_hbm, emb_hbm, near_hbm, far_hbm, gain_ref, col_ref, row_ref,
    qkv_hbm, low_hbm, turned_hbm, mid_ref, n2_ref,
    n1_ref, emb_ref, attn_buf, qkv_buf, low_buf, turned_buf, att_ref, in_sem, low_sem, turned_sem, qkv_sem,
):
    rows, model = n1_ref.shape
    core = lax.rem(lax.axis_index("rows"), 2)
    pairs = (
        (n1_hbm, n1_ref),
        (near_hbm, attn_buf.at[:, core]),
        (far_hbm, attn_buf.at[:, 1 - core]),
        (emb_hbm, emb_ref),
    )
    copies = [pltpu.make_async_copy(*pair, in_sem.at[i]) for i, pair in enumerate(pairs)]
    for copy in copies:
        copy.start()
    for copy in copies:
        copy.wait()
    n1 = n1_ref[...]
    for which in range(3):
        qkv_buf[which] = mm(n1, columns(attn_buf, which, which + 1)).astype(BF16)
    qkv_copy = pltpu.make_async_copy(qkv_buf, qkv_hbm, qkv_sem)
    qkv_copy.start()
    quad = 4 * size
    scale = 1.0 / math.sqrt(size)
    same = col_ref[...] == row_ref[...]

    def low_copy(j):
        part = pl.ds(j * 4, 4)
        return pltpu.make_async_copy(low_buf.at[part], low_hbm.at[part], low_sem.at[j])

    def turned_copy(j):
        part = pl.ds(j * 4, 4)
        return pltpu.make_async_copy(turned_buf.at[part], turned_hbm.at[part], turned_sem.at[j])

    def step(j, carry):
        lanes = pl.ds(pl.multiple_of(j * quad, quad), quad)
        query, keys, vals = qkv_buf[0, :, lanes], qkv_buf[1, :, lanes], qkv_buf[2, :, lanes]
        zero = jnp.zeros_like(query)
        attended = jnp.zeros((rows, quad), F32)
        for head in range(4):
            mask = head_mask((rows, quad), head, size)
            shares = softmax_shares(jnp.where(mask, query, zero), keys, same, scale)
            low = shares.astype(BF16)
            low_buf[j * 4 + head] = low
            turned_buf[j * 4 + head] = shares.T.astype(BF16)
            attended = jnp.where(mask, mm(low, vals), attended)
        att_ref[:, lanes] = attended.astype(BF16)
        low_copy(j).start()
        turned_copy(j).start()
        return carry

    lax.fori_loop(0, model // quad, step, 0)
    mid = emb_ref[...] + mm_nt(att_ref[...], columns(attn_buf, 3, 4))
    mid_ref[...] = mid
    n2_ref[...] = (normalize(mid)[0] * gain_ref[...]).astype(BF16)
    qkv_copy.wait()
    for j in range(model // quad):
        low_copy(j).wait()
        turned_copy(j).wait()


def mlp_kernel(
    n2_hbm, og_hbm, weights_hbm, up_ref, out_ref,
    n2_ref, og_ref, up_buf, down_buf, acc_out, acc_grad, up_sem, down_sem, sem,
):
    chunks, _, width = up_buf.shape

    def up_copy(j):
        start = pl.multiple_of(j * width, width)
        source = weights_hbm.at[:, pl.ds(start, width)]
        return pltpu.make_async_copy(source, up_buf.at[j], up_sem.at[j])

    def down_copy(j):
        start = pl.multiple_of((chunks + j) * width, width)
        source = weights_hbm.at[:, pl.ds(start, width)]
        return pltpu.make_async_copy(source, down_buf.at[j], down_sem.at[j])

    first = pltpu.make_async_copy(n2_hbm, n2_ref, sem.at[0])
    second = pltpu.make_async_copy(og_hbm, og_ref, sem.at[1])
    first.start()
    up_copy(0).start()
    second.start()
    down_copy(0).start()
    for j in range(1, chunks):
        up_copy(j).start()
        down_copy(j).start()
    acc_out[...] = jnp.zeros_like(acc_out)
    acc_grad[...] = jnp.zeros_like(acc_grad)
    first.wait()
    second.wait()

    def step(j, carry):
        up_copy(j).wait()
        pre = mm(n2_ref[...], up_buf[j])
        down_copy(j).wait()
        grad_hidden = mm(og_ref[...], down_buf[j])
        root = math.sqrt(2.0 / math.pi)
        square = pre * pre
        tanh = jnp.tanh(root * pre * (1.0 + 0.044715 * square))
        half = 0.5 * (1.0 + tanh)
        act = (pre * half).astype(BF16)
        slope = half + 0.5 * pre * (1.0 - tanh * tanh) * (root * (1.0 + 3.0 * 0.044715 * square))
        grad_pre = (grad_hidden * slope).astype(BF16)
        acc_grad[...] += mm_nt(grad_pre, up_buf[j])
        acc_out[...] += mm_nt(act, down_buf[j])
        return carry

    lax.fori_loop(0, chunks, step, 0)
    up_ref[...] = acc_grad[...].astype(BF16)
    out_ref[...] = acc_out[...].astype(BF16)


def backward_kernel(
    size, images,
    og_hbm, mid_hbm, mine_hbm, theirs_hbm, near_out_hbm, far_out_hbm, qkv_hbm, low_hbm, turned_hbm,
    near_hbm, far_hbm, emb_hbm, emb_w_hbm, pert_hbm,
    gain1_ref, gain2_ref, ball_ref, col_ref,
    new_ref,
    og_ref, mid_ref, mine_ref, theirs_ref, attn_buf, qkv_buf, low_buf, turned_buf,
    emb_ref, emb_w_ref, pert_ref, acc_grad, heads_ref, proj_ref, sem,
):
    rows, model = og_ref.shape
    core = lax.rem(lax.axis_index("rows"), 2)
    head_part = pl.ds(0, 3 * model)
    out_part = pl.ds(3 * model, model)
    pairs = (
        (og_hbm, og_ref),
        (mid_hbm, mid_ref),
        (mine_hbm, mine_ref),
        (theirs_hbm, theirs_ref),
        (near_out_hbm.at[:, :, out_part], attn_buf.at[:, core, :, out_part]),
        (far_out_hbm.at[:, :, out_part], attn_buf.at[:, 1 - core, :, out_part]),
        (qkv_hbm, qkv_buf),
        (low_hbm, low_buf),
        (turned_hbm, turned_buf),
        (near_hbm.at[:, :, head_part], attn_buf.at[:, core, :, head_part]),
        (far_hbm.at[:, :, head_part], attn_buf.at[:, 1 - core, :, head_part]),
        (emb_hbm, emb_ref),
        (emb_w_hbm, emb_w_ref),
        (pert_hbm, pert_ref),
    )
    copies = [pltpu.make_async_copy(*pair, sem.at[i]) for i, pair in enumerate(pairs)]
    for copy in copies:
        copy.start()
    for copy in copies[:4]:
        copy.wait()
    grad_norm_two = mine_ref[...].astype(F32) + theirs_ref[...].astype(F32)
    grad_mid = og_ref[...].astype(F32) + norm_back(mid_ref[...], gain2_ref[...], grad_norm_two)
    acc_grad[...] = grad_mid
    for copy in copies[4:6]:
        copy.wait()
    heads_ref[...] = mm(grad_mid.astype(BF16), columns(attn_buf, 3, 4)).astype(BF16)
    for copy in copies[6:9]:
        copy.wait()
    quad = 4 * size
    scale = 1.0 / math.sqrt(size)

    def attention_step(j, carry):
        lanes = pl.ds(pl.multiple_of(j * quad, quad), quad)
        query, keys, vals = qkv_buf[0, :, lanes], qkv_buf[1, :, lanes], qkv_buf[2, :, lanes]
        grad_heads = heads_ref[:, lanes]
        zero = jnp.zeros_like(grad_heads)
        grad_query = jnp.zeros((rows, quad), F32)
        grad_keys = jnp.zeros((rows, quad), F32)
        grad_vals = jnp.zeros((rows, quad), F32)
        for head in range(4):
            mask = head_mask((rows, quad), head, size)
            shares = low_buf[j * 4 + head].astype(F32)
            grad_shares = mm_nt(jnp.where(mask, grad_heads, zero), vals)
            grad_vals = jnp.where(mask, mm(turned_buf[j * 4 + head], grad_heads), grad_vals)
            inner = jnp.sum(grad_shares * shares, -1, keepdims=True)
            grad_scores = (shares * (grad_shares - inner) * scale).astype(BF16)
            grad_query = jnp.where(mask, mm(grad_scores, keys), grad_query)
            grad_keys = jnp.where(mask, mm_tn(grad_scores, query), grad_keys)
        for which, value in enumerate((grad_query, grad_keys, grad_vals)):
            start = pl.multiple_of(which * model + j * quad, quad)
            proj_ref[:, pl.ds(start, quad)] = value.astype(BF16)
        return carry

    lax.fori_loop(0, model // quad, attention_step, 0)
    for copy in copies[9:]:
        copy.wait()
    grad_norm = mm_nt(proj_ref[...], columns(attn_buf, 0, 3))
    grad_embed = acc_grad[...] + norm_back(emb_ref[...], gain1_ref[...], grad_norm)
    grad_input = mm_nt(grad_embed.astype(BF16), emb_w_ref[...])
    labels = col_ref[...]
    noise = pert_ref[...]
    patch = noise.shape[1]
    row_sq = jnp.sum(grad_input * grad_input, -1, keepdims=True)
    scale_rows = jnp.zeros_like(row_sq)
    counts = []
    for image in range(images):
        own = labels == image
        count = jnp.sum(jnp.where(own, 1.0, 0.0), 0, keepdims=True) * patch
        counts.append(count)
        total = jnp.sum(jnp.where(own, row_sq, 0.0), 0, keepdims=True)
        scale_rows = jnp.where(own, STEP_SIZE * lax.rsqrt(total / count + 1e-06), scale_rows)
    candidate = noise + scale_rows * grad_input
    row_sq = jnp.sum(candidate * candidate, -1, keepdims=True)
    factor_rows = jnp.zeros_like(row_sq)
    for image in range(images):
        own = labels == image
        total = jnp.sum(jnp.where(own, row_sq, 0.0), 0, keepdims=True)
        factor = jnp.minimum(
            1.0, ball_ref[:, image : image + 1] * lax.rsqrt(total / counts[image] + 1e-06)
        )
        factor_rows = jnp.where(own, factor, factor_rows)
    new_ref[...] = candidate * factor_rows


def block(*shape, dtype=BF16):
    return pltpu.VMEM(shape, dtype)


def params():
    return pltpu.CompilerParams(vmem_limit_bytes=VMEM_LIMIT)


def body(
    pixels,
    perturbation,
    segment_ids,
    ball_radius,
    w_embed,
    gain_attn,
    w_qkv,
    w_out,
    gain_mlp,
    w_up,
    w_down,
    out_grad,
):
    rows, patch = pixels.shape
    model = w_embed.shape[1]
    chunk, _, share = w_qkv.shape
    units = w_up.shape[1]
    size = model // HEADS
    groups = model // share
    images = ball_radius.shape[1]

    mine = jnp.concatenate([w_qkv.reshape(chunk, 3 * share), w_out.T, w_up, w_down.T], 1)
    chunks = lax.all_gather(mine, "heads", axis=0, tiled=False)
    attn = chunks[:, :, : 4 * share].reshape(groups, chunk, 4, share)
    attn = attn.transpose(1, 2, 0, 3).reshape(chunk, 4 * model)
    half = lax.axis_index("heads") % 2
    mlp = chunks[:, :, 4 * share :].reshape(2, groups // 2, chunk, 2, units)
    mlp = lax.dynamic_index_in_dim(mlp, half, 0, keepdims=False)
    mlp = mlp.transpose(1, 2, 0, 3).reshape(chunk, groups * units)
    weights = lax.all_gather(mlp, "rows", axis=0, tiled=True)

    sites = lax.axis_size("rows") // 2
    planes = [[2 * site + core for site in range(sites)] for core in range(2)]
    copies = jnp.broadcast_to(attn[None], (sites,) + attn.shape)
    near = lax.all_to_all(copies, "rows", 0, 0, axis_index_groups=planes)
    near = near.reshape(sites * chunk, 4 * model)
    far = lax.ppermute(near, "rows", [(row, row ^ 1) for row in range(2 * sites)])

    shard = (sites, chunk, 4 * model)
    near, far = near.reshape(shard), far.reshape(shard)

    labels_col = segment_ids.reshape(rows, 1)
    labels_row = segment_ids.reshape(1, rows)
    gain1 = gain_attn.reshape(1, model)
    gain2 = gain_mlp.reshape(1, model)
    quads = model // (4 * size)
    full = lambda dt: jax.ShapeDtypeStruct((rows, model), dt)
    vmem = pl.BlockSpec(memory_space=pltpu.VMEM)
    outside = pl.BlockSpec(memory_space=pl.ANY)
    semaphores = pltpu.SemaphoreType.DMA

    embedded, normed_one = pl.pallas_call(
        embed_kernel,
        in_specs=[vmem] * 4,
        out_specs=[vmem] * 2,
        out_shape=[full(F32), full(BF16)],
        compiler_params=params(),
        cost_estimate=pl.CostEstimate(
            flops=2 * rows * patch * model, bytes_accessed=5 * 1024 * 1024, transcendentals=0
        ),
    )(pixels, perturbation, w_embed, gain1)

    squares = jax.ShapeDtypeStruct((HEADS, rows, rows), BF16)
    qkv, low, turned, stream_mid, normed_two = pl.pallas_call(
        lambda *refs: attention_kernel(size, *refs),
        in_specs=[outside] * 4 + [vmem] * 3,
        out_specs=[outside] * 3 + [vmem] * 2,
        out_shape=[jax.ShapeDtypeStruct((3, rows, model), BF16), squares, squares]
        + [full(F32), full(BF16)],
        scratch_shapes=[
            block(rows, model),
            block(rows, model, dtype=F32),
            block(sites, 2, chunk, 4 * model),
            block(3, rows, model),
            block(HEADS, rows, rows),
            block(HEADS, rows, rows),
            block(rows, model),
            semaphores((4,)),
            semaphores((quads,)),
            semaphores((quads,)),
            semaphores,
        ],
        compiler_params=params(),
    )(normed_one, embedded, near, far, gain2, labels_col, labels_row)

    width = 512
    count = groups * units // 2 // width
    up_mine, out_mine = pl.pallas_call(
        mlp_kernel,
        in_specs=[outside] * 3,
        out_specs=[vmem] * 2,
        out_shape=[full(BF16), full(BF16)],
        scratch_shapes=[
            block(rows, model),
            block(rows, model),
            block(count, model, width),
            block(count, model, width),
            block(rows, model, dtype=F32),
            block(rows, model, dtype=F32),
            semaphores((count,)),
            semaphores((count,)),
            semaphores((2,)),
        ],
        compiler_params=params(),
    )(normed_two, out_grad, weights)

    pairs = [(group, group ^ 1) for group in range(groups)]
    up_theirs = lax.ppermute(up_mine, "heads", pairs)
    out_mine, up_theirs = lax.optimization_barrier((out_mine, up_theirs))
    out_theirs = lax.ppermute(out_mine, "heads", pairs)

    moved = (out_grad, stream_mid, up_mine, up_theirs, near, far, qkv, low, turned)
    moved = moved + (near, far, embedded, w_embed, perturbation)
    updated = pl.pallas_call(
        lambda *refs: backward_kernel(size, images, *refs),
        in_specs=[outside] * len(moved) + [vmem] * 4,
        out_specs=vmem,
        out_shape=jax.ShapeDtypeStruct((rows, patch), F32),
        scratch_shapes=[
            block(rows, model),
            block(rows, model, dtype=F32),
            block(rows, model),
            block(rows, model),
            block(sites, 2, chunk, 4 * model),
            block(3, rows, model),
            block(HEADS, rows, rows),
            block(HEADS, rows, rows),
            block(rows, model, dtype=F32),
            block(patch, model),
            block(rows, patch, dtype=F32),
            block(rows, model, dtype=F32),
            block(rows, model),
            block(rows, 3 * model),
            semaphores((len(moved),)),
        ],
        compiler_params=params(),
        cost_estimate=pl.CostEstimate(
            flops=16 * rows * model * model, bytes_accessed=20 * 1024 * 1024, transcendentals=0
        ),
    )(*moved, gain1, gain2, ball_radius, labels_col)
    block_out = stream_mid + (out_mine.astype(F32) + out_theirs.astype(F32))
    return (block_out.astype(BF16), updated)


def solution(mesh):
    in_specs = (
        P("rows", None),
        P("rows", None),
        P("rows", None),
        P("rows", None),
        P(),
        P(),
        P("rows", None, "heads"),
        P("heads", "rows"),
        P(),
        P("rows", "heads"),
        P("heads", "rows"),
        P("rows", None),
    )
    out_specs = (P("rows", None), P("rows", None))
    return jax.shard_map(body, mesh=mesh, in_specs=in_specs, out_specs=out_specs, check_vma=False)
```

```python
import math

import jax
import jax.numpy as jnp
from jax import lax
from jax.experimental import pallas as pl
from jax.experimental.pallas import tpu as pltpu
from jax.sharding import PartitionSpec as P

HEADS = 16
STEP_SIZE = 0.1
MIB = 1024 * 1024
F32 = jnp.float32
BF16 = jnp.bfloat16


def mm(a, b):
    return lax.dot_general(a, b, (((1,), (0,)), ((), ())), preferred_element_type=F32)


def mm_nt(a, b):
    return lax.dot_general(a, b, (((1,), (1,)), ((), ())), preferred_element_type=F32)


def mm_tn(a, b):
    return lax.dot_general(a, b, (((0,), (0,)), ((), ())), preferred_element_type=F32)


def normalize(values):
    center = jnp.mean(values, -1, keepdims=True)
    shifted = values - center
    spread = jnp.mean(shifted * shifted, -1, keepdims=True)
    inv = lax.rsqrt(spread + 1e-05)
    return shifted * inv, inv


def norm_back(values, gain, upstream):
    hat, inv = normalize(values)
    scaled = upstream * gain
    return inv * (
        scaled
        - jnp.mean(scaled, -1, keepdims=True)
        - hat * jnp.mean(scaled * hat, -1, keepdims=True)
    )


def head_mask(shape, head, size):
    lane = lax.broadcasted_iota(jnp.int32, shape, 1)
    return (lane >= head * size) & (lane < (head + 1) * size)


def softmax_shares(query, keys, same, scale):
    scores = mm_nt(query, keys) * scale
    powers = jnp.where(same, jnp.exp(scores), 0.0)
    return powers * (1.0 / jnp.sum(powers, -1, keepdims=True))


def embed_kernel(pix_ref, pert_ref, weight_ref, gain_ref, emb_ref, n1_ref):
    inputs = (pix_ref[...] + pert_ref[...]).astype(BF16)
    embedded = mm(inputs, weight_ref[...])
    emb_ref[...] = embedded
    n1_ref[...] = (normalize(embedded)[0] * gain_ref[...]).astype(BF16)


def columns(buf, first, last):
    sites, cores, chunk, width = buf.shape
    model = sites * cores * chunk
    return buf[:, :, :, first * model : last * model].reshape(model, (last - first) * model)


def attention_kernel(
    size,
    n1_hbm, emb_hbm, near_hbm, far_hbm, gain_ref, col_ref, row_ref,
    qkv_hbm, low_hbm, turned_hbm, mid_ref, n2_ref,
    n1_ref, emb_ref, attn_buf, qkv_buf, low_buf, turned_buf, att_ref, in_sem, low_sem, turned_sem, qkv_sem,
):
    rows, model = n1_ref.shape
    core = lax.rem(lax.axis_index("rows"), 2)
    pairs = [(n1_hbm, n1_ref)]
    for which in range(4):
        part = pl.ds(which * model, model)
        pairs.append((near_hbm.at[:, :, part], attn_buf.at[:, core, :, part]))
        pairs.append((far_hbm.at[:, :, part], attn_buf.at[:, 1 - core, :, part]))
    pairs.append((emb_hbm, emb_ref))
    copies = [pltpu.make_async_copy(*pair, in_sem.at[i]) for i, pair in enumerate(pairs)]
    for copy in copies:
        copy.start()
    copies[0].wait()
    n1 = n1_ref[...]
    for which in range(3):
        copies[1 + 2 * which].wait()
        copies[2 + 2 * which].wait()
        qkv_buf[which] = mm(n1, columns(attn_buf, which, which + 1)).astype(BF16)
    qkv_copy = pltpu.make_async_copy(qkv_buf, qkv_hbm, qkv_sem)
    qkv_copy.start()
    quad = 4 * size
    scale = 1.0 / math.sqrt(size)
    same = col_ref[...] == row_ref[...]

    def low_copy(j):
        part = pl.ds(j * 4, 4)
        return pltpu.make_async_copy(low_buf.at[part], low_hbm.at[part], low_sem.at[j])

    def turned_copy(j):
        part = pl.ds(j * 4, 4)
        return pltpu.make_async_copy(turned_buf.at[part], turned_hbm.at[part], turned_sem.at[j])

    def step(j, carry):
        lanes = pl.ds(pl.multiple_of(j * quad, quad), quad)
        query, keys, vals = qkv_buf[0, :, lanes], qkv_buf[1, :, lanes], qkv_buf[2, :, lanes]
        zero = jnp.zeros_like(query)
        attended = jnp.zeros((rows, quad), F32)
        for head in range(4):
            mask = head_mask((rows, quad), head, size)
            shares = softmax_shares(jnp.where(mask, query, zero), keys, same, scale)
            low = shares.astype(BF16)
            low_buf[j * 4 + head] = low
            turned_buf[j * 4 + head] = shares.T.astype(BF16)
            attended = jnp.where(mask, mm(low, vals), attended)
        att_ref[:, lanes] = attended.astype(BF16)
        low_copy(j).start()
        turned_copy(j).start()
        return carry

    lax.fori_loop(0, model // quad, step, 0)
    for copy in copies[7:]:
        copy.wait()
    mid = emb_ref[...] + mm_nt(att_ref[...], columns(attn_buf, 3, 4))
    mid_ref[...] = mid
    n2_ref[...] = (normalize(mid)[0] * gain_ref[...]).astype(BF16)
    qkv_copy.wait()
    for j in range(model // quad):
        low_copy(j).wait()
        turned_copy(j).wait()


def mlp_kernel(
    n2_hbm, og_hbm, weights_hbm, up_ref, out_ref,
    n2_ref, og_ref, up_buf, down_buf, acc_out, acc_grad, up_sem, down_sem, sem,
):
    chunks, _, width = up_buf.shape

    def up_copy(j):
        start = pl.multiple_of(j * width, width)
        source = weights_hbm.at[:, pl.ds(start, width)]
        return pltpu.make_async_copy(source, up_buf.at[j], up_sem.at[j])

    def down_copy(j):
        start = pl.multiple_of((chunks + j) * width, width)
        source = weights_hbm.at[:, pl.ds(start, width)]
        return pltpu.make_async_copy(source, down_buf.at[j], down_sem.at[j])

    first = pltpu.make_async_copy(n2_hbm, n2_ref, sem.at[0])
    second = pltpu.make_async_copy(og_hbm, og_ref, sem.at[1])
    first.start()
    up_copy(0).start()
    second.start()
    down_copy(0).start()
    for j in range(1, chunks):
        up_copy(j).start()
        down_copy(j).start()
    acc_out[...] = jnp.zeros_like(acc_out)
    acc_grad[...] = jnp.zeros_like(acc_grad)
    first.wait()
    second.wait()

    def front(j):
        up_copy(j).wait()
        pre = mm(n2_ref[...], up_buf[j])
        down_copy(j).wait()
        return pre, mm(og_ref[...], down_buf[j])

    def back(j, pre, grad_hidden):
        root = math.sqrt(2.0 / math.pi)
        square = pre * pre
        tanh = jnp.tanh(root * pre * (1.0 + 0.044715 * square))
        half = 0.5 * (1.0 + tanh)
        act = (pre * half).astype(BF16)
        slope = half + 0.5 * pre * (1.0 - tanh * tanh) * (root * (1.0 + 3.0 * 0.044715 * square))
        grad_pre = (grad_hidden * slope).astype(BF16)
        acc_grad[...] += mm_nt(grad_pre, up_buf[j])
        acc_out[...] += mm_nt(act, down_buf[j])

    now = front(0)
    for j in range(chunks):
        later = front(j + 1) if j + 1 < chunks else None
        back(j, *now)
        now = later
    up_ref[...] = acc_grad[...].astype(BF16)
    out_ref[...] = acc_out[...].astype(BF16)


def backward_kernel(
    size, images,
    near_hbm, far_hbm,
    og_ref, mid_ref, mine_ref, theirs_ref, qkv_buf, low_buf, turned_buf,
    emb_ref, emb_w_ref, pert_ref, gain1_ref, gain2_ref, ball_ref, col_ref,
    new_ref,
    attn_buf, acc_grad, heads_ref, proj_ref, sem,
):
    rows, model = og_ref.shape
    core = lax.rem(lax.axis_index("rows"), 2)
    head_part = pl.ds(0, 3 * model)
    out_part = pl.ds(3 * model, model)
    pairs = (
        (near_hbm.at[:, :, out_part], attn_buf.at[:, core, :, out_part]),
        (far_hbm.at[:, :, out_part], attn_buf.at[:, 1 - core, :, out_part]),
        (near_hbm.at[:, :, head_part], attn_buf.at[:, core, :, head_part]),
        (far_hbm.at[:, :, head_part], attn_buf.at[:, 1 - core, :, head_part]),
    )
    copies = [pltpu.make_async_copy(*pair, sem.at[i]) for i, pair in enumerate(pairs)]
    for copy in copies:
        copy.start()
    grad_norm_two = mine_ref[...].astype(F32) + theirs_ref[...].astype(F32)
    grad_mid = og_ref[...].astype(F32) + norm_back(mid_ref[...], gain2_ref[...], grad_norm_two)
    acc_grad[...] = grad_mid
    for copy in copies[:2]:
        copy.wait()
    heads_ref[...] = mm(grad_mid.astype(BF16), columns(attn_buf, 3, 4)).astype(BF16)
    quad = 4 * size
    scale = 1.0 / math.sqrt(size)

    def attention_step(j, carry):
        lanes = pl.ds(pl.multiple_of(j * quad, quad), quad)
        query, keys, vals = qkv_buf[0, :, lanes], qkv_buf[1, :, lanes], qkv_buf[2, :, lanes]
        grad_heads = heads_ref[:, lanes]
        zero = jnp.zeros_like(grad_heads)
        grad_query = jnp.zeros((rows, quad), F32)
        grad_keys = jnp.zeros((rows, quad), F32)
        grad_vals = jnp.zeros((rows, quad), F32)
        for head in range(4):
            mask = head_mask((rows, quad), head, size)
            shares = low_buf[j * 4 + head].astype(F32)
            grad_shares = mm_nt(jnp.where(mask, grad_heads, zero), vals)
            grad_vals = jnp.where(mask, mm(turned_buf[j * 4 + head], grad_heads), grad_vals)
            inner = jnp.sum(grad_shares * shares, -1, keepdims=True)
            grad_scores = (shares * (grad_shares - inner) * scale).astype(BF16)
            grad_query = jnp.where(mask, mm(grad_scores, keys), grad_query)
            grad_keys = jnp.where(mask, mm_tn(grad_scores, query), grad_keys)
        for which, value in enumerate((grad_query, grad_keys, grad_vals)):
            start = pl.multiple_of(which * model + j * quad, quad)
            proj_ref[:, pl.ds(start, quad)] = value.astype(BF16)
        return carry

    lax.fori_loop(0, model // quad, attention_step, 0)
    for copy in copies[2:]:
        copy.wait()
    grad_norm = mm_nt(proj_ref[...], columns(attn_buf, 0, 3))
    grad_embed = acc_grad[...] + norm_back(emb_ref[...], gain1_ref[...], grad_norm)
    grad_input = mm_nt(grad_embed.astype(BF16), emb_w_ref[...])
    labels = col_ref[...]
    noise = pert_ref[...]
    patch = noise.shape[1]
    row_sq = jnp.sum(grad_input * grad_input, -1, keepdims=True)
    scale_rows = jnp.zeros_like(row_sq)
    counts = []
    for image in range(images):
        own = labels == image
        count = jnp.sum(jnp.where(own, 1.0, 0.0), 0, keepdims=True) * patch
        counts.append(count)
        total = jnp.sum(jnp.where(own, row_sq, 0.0), 0, keepdims=True)
        scale_rows = jnp.where(own, STEP_SIZE * lax.rsqrt(total / count + 1e-06), scale_rows)
    candidate = noise + scale_rows * grad_input
    row_sq = jnp.sum(candidate * candidate, -1, keepdims=True)
    factor_rows = jnp.zeros_like(row_sq)
    for image in range(images):
        own = labels == image
        total = jnp.sum(jnp.where(own, row_sq, 0.0), 0, keepdims=True)
        factor = jnp.minimum(
            1.0, ball_ref[:, image : image + 1] * lax.rsqrt(total / counts[image] + 1e-06)
        )
        factor_rows = jnp.where(own, factor, factor_rows)
    new_ref[...] = candidate * factor_rows


def block(*shape, dtype=BF16):
    return pltpu.VMEM(shape, dtype)


def params(mib):
    return pltpu.CompilerParams(vmem_limit_bytes=mib * MIB)


def body(
    pixels,
    perturbation,
    segment_ids,
    ball_radius,
    w_embed,
    gain_attn,
    w_qkv,
    w_out,
    gain_mlp,
    w_up,
    w_down,
    out_grad,
):
    rows, patch = pixels.shape
    model = w_embed.shape[1]
    chunk, _, share = w_qkv.shape
    units = w_up.shape[1]
    size = model // HEADS
    groups = model // share
    images = ball_radius.shape[1]

    mine = jnp.concatenate([w_qkv.reshape(chunk, 3 * share), w_out.T, w_up, w_down.T], 1)
    chunks = lax.all_gather(mine, "heads", axis=0, tiled=False)
    attn = chunks[:, :, : 4 * share].reshape(groups, chunk, 4, share)
    attn = attn.transpose(1, 2, 0, 3).reshape(chunk, 4 * model)
    half = lax.axis_index("heads") % 2
    mlp = chunks[:, :, 4 * share :].reshape(2, groups // 2, chunk, 2, units)
    mlp = lax.dynamic_index_in_dim(mlp, half, 0, keepdims=False)
    mlp = mlp.transpose(1, 2, 0, 3).reshape(chunk, groups * units)
    weights = lax.all_gather(mlp, "rows", axis=0, tiled=True)

    sites = lax.axis_size("rows") // 2
    planes = [[2 * site + core for site in range(sites)] for core in range(2)]
    copies = jnp.broadcast_to(attn[None], (sites,) + attn.shape)
    near = lax.all_to_all(copies, "rows", 0, 0, axis_index_groups=planes)
    near = near.reshape(sites * chunk, 4 * model)
    far = lax.ppermute(near, "rows", [(row, row ^ 1) for row in range(2 * sites)])

    shard = (sites, chunk, 4 * model)
    near, far = near.reshape(shard), far.reshape(shard)

    labels_col = segment_ids.reshape(rows, 1)
    labels_row = segment_ids.reshape(1, rows)
    gain1 = gain_attn.reshape(1, model)
    gain2 = gain_mlp.reshape(1, model)
    quads = model // (4 * size)
    full = lambda dt: jax.ShapeDtypeStruct((rows, model), dt)
    vmem = pl.BlockSpec(memory_space=pltpu.VMEM)
    outside = pl.BlockSpec(memory_space=pl.ANY)
    semaphores = pltpu.SemaphoreType.DMA

    embedded, normed_one = pl.pallas_call(
        embed_kernel,
        in_specs=[vmem] * 4,
        out_specs=[vmem] * 2,
        out_shape=[full(F32), full(BF16)],
        compiler_params=params(12),
        cost_estimate=pl.CostEstimate(
            flops=2 * rows * patch * model, bytes_accessed=5 * 1024 * 1024, transcendentals=0
        ),
    )(pixels, perturbation, w_embed, gain1)

    squares = jax.ShapeDtypeStruct((HEADS, rows, rows), BF16)
    qkv, low, turned, stream_mid, normed_two = pl.pallas_call(
        lambda *refs: attention_kernel(size, *refs),
        in_specs=[outside] * 4 + [vmem] * 3,
        out_specs=[outside] * 3 + [vmem] * 2,
        out_shape=[jax.ShapeDtypeStruct((3, rows, model), BF16), squares, squares]
        + [full(F32), full(BF16)],
        scratch_shapes=[
            block(rows, model),
            block(rows, model, dtype=F32),
            block(sites, 2, chunk, 4 * model),
            block(3, rows, model),
            block(HEADS, rows, rows),
            block(HEADS, rows, rows),
            block(rows, model),
            semaphores((10,)),
            semaphores((quads,)),
            semaphores((quads,)),
            semaphores,
        ],
        compiler_params=params(56),
    )(normed_one, embedded, near, far, gain2, labels_col, labels_row)

    width = 1024
    count = groups * units // 2 // width
    up_mine, out_mine = pl.pallas_call(
        mlp_kernel,
        in_specs=[outside] * 3,
        out_specs=[vmem] * 2,
        out_shape=[full(BF16), full(BF16)],
        scratch_shapes=[
            block(rows, model),
            block(rows, model),
            block(count, model, width),
            block(count, model, width),
            block(rows, model, dtype=F32),
            block(rows, model, dtype=F32),
            semaphores((count,)),
            semaphores((count,)),
            semaphores((2,)),
        ],
        compiler_params=params(49),
    )(normed_two, out_grad, weights)

    pairs = [(group, group ^ 1) for group in range(groups)]
    up_theirs = lax.ppermute(up_mine, "heads", pairs)
    out_theirs = lax.ppermute(out_mine, "heads", pairs)

    held = (out_grad, stream_mid, up_mine, up_theirs, qkv, low, turned, embedded, w_embed)
    held = held + (perturbation, gain1, gain2, ball_radius, labels_col)
    updated = pl.pallas_call(
        lambda *refs: backward_kernel(size, images, *refs),
        in_specs=[outside] * 2 + [vmem] * len(held),
        out_specs=vmem,
        out_shape=jax.ShapeDtypeStruct((rows, patch), F32),
        scratch_shapes=[
            block(sites, 2, chunk, 4 * model),
            block(rows, model, dtype=F32),
            block(rows, model),
            block(rows, 3 * model),
            semaphores((4,)),
        ],
        compiler_params=params(30),
        cost_estimate=pl.CostEstimate(
            flops=16 * rows * model * model, bytes_accessed=20 * 1024 * 1024, transcendentals=0
        ),
    )(near, far, *held)
    out_theirs, updated = lax.optimization_barrier((out_theirs, updated))
    block_out = stream_mid + (out_mine.astype(F32) + out_theirs.astype(F32))
    return (block_out.astype(BF16), updated)


def solution(mesh):
    in_specs = (
        P("rows", None),
        P("rows", None),
        P("rows", None),
        P("rows", None),
        P(),
        P(),
        P("rows", None, "heads"),
        P("heads", "rows"),
        P(),
        P("rows", "heads"),
        P("heads", "rows"),
        P("rows", None),
    )
    out_specs = (P("rows", None), P("rows", None))
    return jax.shard_map(body, mesh=mesh, in_specs=in_specs, out_specs=out_specs, check_vma=False)
```

```python
import math

import jax
import jax.numpy as jnp
from jax import lax
from jax.experimental import pallas as pl
from jax.experimental.pallas import tpu as pltpu
from jax.sharding import PartitionSpec as P

HEADS = 16
STEP_SIZE = 0.1
MIB = 1024 * 1024
F32 = jnp.float32
BF16 = jnp.bfloat16


def mm(a, b):
    return lax.dot_general(a, b, (((1,), (0,)), ((), ())), preferred_element_type=F32)


def mm_nt(a, b):
    return lax.dot_general(a, b, (((1,), (1,)), ((), ())), preferred_element_type=F32)


def mm_tn(a, b):
    return lax.dot_general(a, b, (((0,), (0,)), ((), ())), preferred_element_type=F32)


def normalize(values):
    center = jnp.mean(values, -1, keepdims=True)
    shifted = values - center
    spread = jnp.mean(shifted * shifted, -1, keepdims=True)
    inv = lax.rsqrt(spread + 1e-05)
    return shifted * inv, inv


def norm_back(values, gain, upstream):
    hat, inv = normalize(values)
    scaled = upstream * gain
    return inv * (
        scaled
        - jnp.mean(scaled, -1, keepdims=True)
        - hat * jnp.mean(scaled * hat, -1, keepdims=True)
    )


def head_mask(shape, head, size):
    lane = lax.broadcasted_iota(jnp.int32, shape, 1)
    return (lane >= head * size) & (lane < (head + 1) * size)


def softmax_shares(query, keys, same, scale):
    scores = mm_nt(query, keys) * scale
    powers = jnp.where(same, jnp.exp(scores), 0.0)
    return powers * (1.0 / jnp.sum(powers, -1, keepdims=True))


def embed_kernel(pix_ref, pert_ref, weight_ref, gain_ref, emb_ref, n1_ref):
    inputs = (pix_ref[...] + pert_ref[...]).astype(BF16)
    embedded = mm(inputs, weight_ref[...])
    emb_ref[...] = embedded
    n1_ref[...] = (normalize(embedded)[0] * gain_ref[...]).astype(BF16)


def columns(buf, first, last):
    sites, cores, chunk, width = buf.shape
    model = sites * cores * chunk
    return buf[:, :, :, first * model : last * model].reshape(model, (last - first) * model)


def attention_kernel(
    size,
    n1_hbm, emb_hbm, near_hbm, far_hbm, gain_ref, col_ref, row_ref,
    qkv_hbm, low_hbm, turned_hbm, mid_ref, n2_ref,
    n1_ref, emb_ref, attn_buf, qkv_buf, low_buf, turned_buf, att_ref, in_sem, low_sem, turned_sem, qkv_sem,
):
    rows, model = n1_ref.shape
    core = lax.rem(lax.axis_index("rows"), 2)
    pairs = [(n1_hbm, n1_ref)]
    for which in range(4):
        part = pl.ds(which * model, model)
        pairs.append((near_hbm.at[:, :, part], attn_buf.at[:, core, :, part]))
        pairs.append((far_hbm.at[:, :, part], attn_buf.at[:, 1 - core, :, part]))
    pairs.append((emb_hbm, emb_ref))
    copies = [pltpu.make_async_copy(*pair, in_sem.at[i]) for i, pair in enumerate(pairs)]
    for copy in copies:
        copy.start()
    copies[0].wait()
    n1 = n1_ref[...]
    for which in range(3):
        copies[1 + 2 * which].wait()
        copies[2 + 2 * which].wait()
        qkv_buf[which] = mm(n1, columns(attn_buf, which, which + 1)).astype(BF16)
    qkv_copy = pltpu.make_async_copy(qkv_buf, qkv_hbm, qkv_sem)
    qkv_copy.start()
    quad = 4 * size
    scale = 1.0 / math.sqrt(size)
    same = col_ref[...] == row_ref[...]

    def low_copy(j):
        part = pl.ds(j * 4, 4)
        return pltpu.make_async_copy(low_buf.at[part], low_hbm.at[part], low_sem.at[j])

    def turned_copy(j):
        part = pl.ds(j * 4, 4)
        return pltpu.make_async_copy(turned_buf.at[part], turned_hbm.at[part], turned_sem.at[j])

    def step(j, carry):
        lanes = pl.ds(pl.multiple_of(j * quad, quad), quad)
        query, keys, vals = qkv_buf[0, :, lanes], qkv_buf[1, :, lanes], qkv_buf[2, :, lanes]
        zero = jnp.zeros_like(query)
        attended = jnp.zeros((rows, quad), F32)
        for head in range(4):
            mask = head_mask((rows, quad), head, size)
            shares = softmax_shares(jnp.where(mask, query, zero), keys, same, scale)
            low = shares.astype(BF16)
            low_buf[j * 4 + head] = low
            turned_buf[j * 4 + head] = shares.T.astype(BF16)
            attended = jnp.where(mask, mm(low, vals), attended)
        att_ref[:, lanes] = attended.astype(BF16)
        low_copy(j).start()
        turned_copy(j).start()
        return carry

    lax.fori_loop(0, model // quad, step, 0)
    for copy in copies[7:]:
        copy.wait()
    mid = emb_ref[...] + mm_nt(att_ref[...], columns(attn_buf, 3, 4))
    mid_ref[...] = mid
    n2_ref[...] = (normalize(mid)[0] * gain_ref[...]).astype(BF16)
    qkv_copy.wait()
    for j in range(model // quad):
        low_copy(j).wait()
        turned_copy(j).wait()


def mlp_kernel(
    n2_hbm, og_hbm, weights_hbm, top_ref, low_ref, out_ref,
    n2_ref, og_ref, up_buf, down_buf, acc_out, acc_grad, up_sem, down_sem, sem,
):
    chunks, _, width = up_buf.shape

    def up_copy(j):
        start = pl.multiple_of(j * width, width)
        source = weights_hbm.at[:, pl.ds(start, width)]
        return pltpu.make_async_copy(source, up_buf.at[j], up_sem.at[j])

    def down_copy(j):
        start = pl.multiple_of((chunks + j) * width, width)
        source = weights_hbm.at[:, pl.ds(start, width)]
        return pltpu.make_async_copy(source, down_buf.at[j], down_sem.at[j])

    first = pltpu.make_async_copy(n2_hbm, n2_ref, sem.at[0])
    second = pltpu.make_async_copy(og_hbm, og_ref, sem.at[1])
    first.start()
    up_copy(0).start()
    second.start()
    down_copy(0).start()
    for j in range(1, chunks):
        up_copy(j).start()
        down_copy(j).start()
    acc_out[...] = jnp.zeros_like(acc_out)
    acc_grad[...] = jnp.zeros_like(acc_grad)
    first.wait()
    second.wait()

    def front(j):
        up_copy(j).wait()
        pre = mm(n2_ref[...], up_buf[j])
        down_copy(j).wait()
        return pre, mm(og_ref[...], down_buf[j])

    def back(j, pre, grad_hidden):
        root = math.sqrt(2.0 / math.pi)
        square = pre * pre
        tanh = jnp.tanh(root * pre * (1.0 + 0.044715 * square))
        half = 0.5 * (1.0 + tanh)
        act = (pre * half).astype(BF16)
        slope = half + 0.5 * pre * (1.0 - tanh * tanh) * (root * (1.0 + 3.0 * 0.044715 * square))
        grad_pre = (grad_hidden * slope).astype(BF16)
        acc_grad[...] += mm_nt(grad_pre, up_buf[j])
        acc_out[...] += mm_nt(act, down_buf[j])

    now = front(0)
    for j in range(chunks):
        later = front(j + 1) if j + 1 < chunks else None
        back(j, *now)
        now = later
    middle = top_ref.shape[0]
    top_ref[...] = acc_grad[:middle].astype(BF16)
    low_ref[...] = acc_grad[middle:].astype(BF16)
    out_ref[...] = acc_out[...].astype(BF16)


def backward_kernel(
    size, images,
    attn_buf,
    og_ref, mid_ref, top_mine_ref, top_theirs_ref, low_mine_ref, low_theirs_ref, qkv_buf, low_buf, turned_buf,
    emb_ref, emb_w_ref, pert_ref, gain1_ref, gain2_ref, ball_ref, col_ref,
    new_ref,
    acc_grad, heads_ref, proj_ref,
):
    rows, model = og_ref.shape
    middle = rows // 2
    for part, mine, theirs in (
        (slice(0, middle), top_mine_ref, top_theirs_ref),
        (slice(middle, rows), low_mine_ref, low_theirs_ref),
    ):
        grad_norm_two = mine[...].astype(F32) + theirs[...].astype(F32)
        acc_grad[part] = og_ref[part].astype(F32) + norm_back(
            mid_ref[part], gain2_ref[...], grad_norm_two
        )
    grad_mid = acc_grad[...]
    heads_ref[...] = mm(grad_mid.astype(BF16), columns(attn_buf, 3, 4)).astype(BF16)
    quad = 4 * size
    scale = 1.0 / math.sqrt(size)

    def attention_step(j, carry):
        lanes = pl.ds(pl.multiple_of(j * quad, quad), quad)
        query, keys, vals = qkv_buf[0, :, lanes], qkv_buf[1, :, lanes], qkv_buf[2, :, lanes]
        grad_heads = heads_ref[:, lanes]
        zero = jnp.zeros_like(grad_heads)
        grad_query = jnp.zeros((rows, quad), F32)
        grad_keys = jnp.zeros((rows, quad), F32)
        grad_vals = jnp.zeros((rows, quad), F32)
        for head in range(4):
            mask = head_mask((rows, quad), head, size)
            shares = low_buf[j * 4 + head].astype(F32)
            grad_shares = mm_nt(jnp.where(mask, grad_heads, zero), vals)
            grad_vals = jnp.where(mask, mm(turned_buf[j * 4 + head], grad_heads), grad_vals)
            inner = jnp.sum(grad_shares * shares, -1, keepdims=True)
            grad_scores = (shares * (grad_shares - inner) * scale).astype(BF16)
            grad_query = jnp.where(mask, mm(grad_scores, keys), grad_query)
            grad_keys = jnp.where(mask, mm_tn(grad_scores, query), grad_keys)
        for which, value in enumerate((grad_query, grad_keys, grad_vals)):
            start = pl.multiple_of(which * model + j * quad, quad)
            proj_ref[:, pl.ds(start, quad)] = value.astype(BF16)
        return carry

    lax.fori_loop(0, model // quad, attention_step, 0)
    grad_norm = mm_nt(proj_ref[...], columns(attn_buf, 0, 3))
    grad_embed = acc_grad[...] + norm_back(emb_ref[...], gain1_ref[...], grad_norm)
    grad_input = mm_nt(grad_embed.astype(BF16), emb_w_ref[...])
    labels = col_ref[...]
    noise = pert_ref[...]
    patch = noise.shape[1]
    row_sq = jnp.sum(grad_input * grad_input, -1, keepdims=True)
    scale_rows = jnp.zeros_like(row_sq)
    counts = []
    for image in range(images):
        own = labels == image
        count = jnp.sum(jnp.where(own, 1.0, 0.0), 0, keepdims=True) * patch
        counts.append(count)
        total = jnp.sum(jnp.where(own, row_sq, 0.0), 0, keepdims=True)
        scale_rows = jnp.where(own, STEP_SIZE * lax.rsqrt(total / count + 1e-06), scale_rows)
    candidate = noise + scale_rows * grad_input
    row_sq = jnp.sum(candidate * candidate, -1, keepdims=True)
    factor_rows = jnp.zeros_like(row_sq)
    for image in range(images):
        own = labels == image
        total = jnp.sum(jnp.where(own, row_sq, 0.0), 0, keepdims=True)
        factor = jnp.minimum(
            1.0, ball_ref[:, image : image + 1] * lax.rsqrt(total / counts[image] + 1e-06)
        )
        factor_rows = jnp.where(own, factor, factor_rows)
    new_ref[...] = candidate * factor_rows


def place_kernel(near_hbm, far_hbm, placed_ref, sem):
    core = lax.rem(lax.axis_index("rows"), 2)
    first = pltpu.make_async_copy(near_hbm, placed_ref.at[:, core], sem.at[0])
    second = pltpu.make_async_copy(far_hbm, placed_ref.at[:, 1 - core], sem.at[1])
    first.start()
    second.start()
    first.wait()
    second.wait()


def block(*shape, dtype=BF16):
    return pltpu.VMEM(shape, dtype)


def params(mib):
    return pltpu.CompilerParams(vmem_limit_bytes=mib * MIB)


def body(
    pixels,
    perturbation,
    segment_ids,
    ball_radius,
    w_embed,
    gain_attn,
    w_qkv,
    w_out,
    gain_mlp,
    w_up,
    w_down,
    out_grad,
):
    rows, patch = pixels.shape
    model = w_embed.shape[1]
    chunk, _, share = w_qkv.shape
    units = w_up.shape[1]
    size = model // HEADS
    groups = model // share
    images = ball_radius.shape[1]

    mine = jnp.concatenate([w_qkv.reshape(chunk, 3 * share), w_out.T, w_up, w_down.T], 1)
    chunks = lax.all_gather(mine, "heads", axis=0, tiled=False)
    attn = chunks[:, :, : 4 * share].reshape(groups, chunk, 4, share)
    attn = attn.transpose(1, 2, 0, 3).reshape(chunk, 4 * model)
    half = lax.axis_index("heads") % 2
    mlp = chunks[:, :, 4 * share :].reshape(2, groups // 2, chunk, 2, units)
    mlp = lax.dynamic_index_in_dim(mlp, half, 0, keepdims=False)
    mlp = mlp.transpose(1, 2, 0, 3).reshape(chunk, groups * units)
    weights = lax.all_gather(mlp, "rows", axis=0, tiled=True)

    sites = lax.axis_size("rows") // 2
    planes = [[2 * site + core for site in range(sites)] for core in range(2)]
    copies = jnp.broadcast_to(attn[None], (sites,) + attn.shape)
    near = lax.all_to_all(copies, "rows", 0, 0, axis_index_groups=planes)
    near = near.reshape(sites * chunk, 4 * model)
    far = lax.ppermute(near, "rows", [(row, row ^ 1) for row in range(2 * sites)])

    shard = (sites, chunk, 4 * model)
    near, far = near.reshape(shard), far.reshape(shard)

    labels_col = segment_ids.reshape(rows, 1)
    labels_row = segment_ids.reshape(1, rows)
    gain1 = gain_attn.reshape(1, model)
    gain2 = gain_mlp.reshape(1, model)
    quads = model // (4 * size)
    full = lambda dt: jax.ShapeDtypeStruct((rows, model), dt)
    vmem = pl.BlockSpec(memory_space=pltpu.VMEM)
    outside = pl.BlockSpec(memory_space=pl.ANY)
    semaphores = pltpu.SemaphoreType.DMA

    embedded, normed_one = pl.pallas_call(
        embed_kernel,
        in_specs=[vmem] * 4,
        out_specs=[vmem] * 2,
        out_shape=[full(F32), full(BF16)],
        compiler_params=params(12),
        cost_estimate=pl.CostEstimate(
            flops=2 * rows * patch * model, bytes_accessed=5 * 1024 * 1024, transcendentals=0
        ),
    )(pixels, perturbation, w_embed, gain1)

    squares = jax.ShapeDtypeStruct((HEADS, rows, rows), BF16)
    qkv, low, turned, stream_mid, normed_two = pl.pallas_call(
        lambda *refs: attention_kernel(size, *refs),
        in_specs=[outside] * 4 + [vmem] * 3,
        out_specs=[outside] * 3 + [vmem] * 2,
        out_shape=[jax.ShapeDtypeStruct((3, rows, model), BF16), squares, squares]
        + [full(F32), full(BF16)],
        scratch_shapes=[
            block(rows, model),
            block(rows, model, dtype=F32),
            block(sites, 2, chunk, 4 * model),
            block(3, rows, model),
            block(HEADS, rows, rows),
            block(HEADS, rows, rows),
            block(rows, model),
            semaphores((10,)),
            semaphores((quads,)),
            semaphores((quads,)),
            semaphores,
        ],
        compiler_params=params(56),
    )(normed_one, embedded, near, far, gain2, labels_col, labels_row)

    width = 1024
    count = groups * units // 2 // width
    half_rows = jax.ShapeDtypeStruct((rows // 2, model), BF16)
    top_mine, low_mine, out_mine = pl.pallas_call(
        mlp_kernel,
        in_specs=[outside] * 3,
        out_specs=[vmem] * 3,
        out_shape=[half_rows, half_rows, full(BF16)],
        scratch_shapes=[
            block(rows, model),
            block(rows, model),
            block(count, model, width),
            block(count, model, width),
            block(rows, model, dtype=F32),
            block(rows, model, dtype=F32),
            semaphores((count,)),
            semaphores((count,)),
            semaphores((2,)),
        ],
        compiler_params=params(49),
    )(normed_two, out_grad, weights)

    down = [(group, (group - 1) % groups) for group in range(groups)]
    above = [(group, (group + 1) % groups) for group in range(groups)]
    top_theirs = lax.ppermute(top_mine, "heads", down)
    low_theirs = lax.ppermute(low_mine, "heads", above)
    out_theirs = lax.ppermute(out_mine, "heads", [(group, group ^ 1) for group in range(groups)])
    near, far, _ = lax.optimization_barrier((near, far, top_mine))
    placed = pl.pallas_call(
        place_kernel,
        in_specs=[outside] * 2,
        out_specs=vmem,
        out_shape=jax.ShapeDtypeStruct((sites, 2, chunk, 4 * model), BF16),
        scratch_shapes=[semaphores((2,))],
        compiler_params=params(20),
        cost_estimate=pl.CostEstimate(flops=0, bytes_accessed=8 * MIB, transcendentals=0),
    )(near, far)

    held = (placed, out_grad, stream_mid, top_mine, top_theirs, low_mine, low_theirs)
    held = held + (qkv, low, turned, embedded, w_embed)
    held = held + (perturbation, gain1, gain2, ball_radius, labels_col)
    updated = pl.pallas_call(
        lambda *refs: backward_kernel(size, images, *refs),
        in_specs=[vmem] * len(held),
        out_specs=vmem,
        out_shape=jax.ShapeDtypeStruct((rows, patch), F32),
        scratch_shapes=[
            block(rows, model, dtype=F32),
            block(rows, model),
            block(rows, 3 * model),
        ],
        compiler_params=params(24),
        cost_estimate=pl.CostEstimate(
            flops=16 * rows * model * model, bytes_accessed=20 * 1024 * 1024, transcendentals=0
        ),
    )(*held)
    out_theirs, updated = lax.optimization_barrier((out_theirs, updated))
    block_out = stream_mid + (out_mine.astype(F32) + out_theirs.astype(F32))
    return (block_out.astype(BF16), updated)


def solution(mesh):
    in_specs = (
        P("rows", None),
        P("rows", None),
        P("rows", None),
        P("rows", None),
        P(),
        P(),
        P("rows", None, "heads"),
        P("heads", "rows"),
        P(),
        P("rows", "heads"),
        P("heads", "rows"),
        P("rows", None),
    )
    out_specs = (P("rows", None), P("rows", None))
    return jax.shard_map(body, mesh=mesh, in_specs=in_specs, out_specs=out_specs, check_vma=False)
```

```python
import math

import jax
import jax.numpy as jnp
from jax import lax
from jax.experimental import pallas as pl
from jax.experimental.pallas import tpu as pltpu
from jax.sharding import PartitionSpec as P

HEADS = 16
STEP_SIZE = 0.1
MIB = 1024 * 1024
F32 = jnp.float32
BF16 = jnp.bfloat16


def mm(a, b):
    return lax.dot_general(a, b, (((1,), (0,)), ((), ())), preferred_element_type=F32)


def mm_nt(a, b):
    return lax.dot_general(a, b, (((1,), (1,)), ((), ())), preferred_element_type=F32)


def mm_tn(a, b):
    return lax.dot_general(a, b, (((0,), (0,)), ((), ())), preferred_element_type=F32)


def normalize(values):
    center = jnp.mean(values, -1, keepdims=True)
    shifted = values - center
    spread = jnp.mean(shifted * shifted, -1, keepdims=True)
    inv = lax.rsqrt(spread + 1e-05)
    return shifted * inv, inv


def norm_back(values, gain, upstream):
    hat, inv = normalize(values)
    scaled = upstream * gain
    return inv * (
        scaled
        - jnp.mean(scaled, -1, keepdims=True)
        - hat * jnp.mean(scaled * hat, -1, keepdims=True)
    )


def head_mask(shape, head, size):
    lane = lax.broadcasted_iota(jnp.int32, shape, 1)
    return (lane >= head * size) & (lane < (head + 1) * size)


def softmax_shares(query, keys, same, scale):
    scores = mm_nt(query, keys) * scale
    powers = jnp.where(same, jnp.exp(scores), 0.0)
    return powers * (1.0 / jnp.sum(powers, -1, keepdims=True))


def embed_kernel(pix_ref, pert_ref, weight_ref, gain_ref, emb_ref, n1_ref):
    inputs = (pix_ref[...] + pert_ref[...]).astype(BF16)
    embedded = mm(inputs, weight_ref[...])
    emb_ref[...] = embedded
    n1_ref[...] = (normalize(embedded)[0] * gain_ref[...]).astype(BF16)


def columns(buf, first, last):
    sites, cores, chunk, width = buf.shape
    model = sites * cores * chunk
    return buf[:, :, :, first * model : last * model].reshape(model, (last - first) * model)


def attention_kernel(
    size,
    n1_hbm, emb_hbm, near_hbm, far_hbm, gain_ref, col_ref, row_ref,
    qkv_hbm, low_hbm, turned_hbm, mid_ref, n2_ref,
    n1_ref, emb_ref, attn_buf, qkv_buf, low_buf, turned_buf, att_ref, in_sem, low_sem, turned_sem, qkv_sem,
):
    rows, model = n1_ref.shape
    core = lax.rem(lax.axis_index("rows"), 2)
    pairs = [(n1_hbm, n1_ref)]
    for which in range(4):
        part = pl.ds(which * model, model)
        pairs.append((near_hbm.at[:, :, part], attn_buf.at[:, core, :, part]))
        pairs.append((far_hbm.at[:, :, part], attn_buf.at[:, 1 - core, :, part]))
    pairs.append((emb_hbm, emb_ref))
    copies = [pltpu.make_async_copy(*pair, in_sem.at[i]) for i, pair in enumerate(pairs)]
    for copy in copies:
        copy.start()
    copies[0].wait()
    n1 = n1_ref[...]
    for which in range(3):
        copies[1 + 2 * which].wait()
        copies[2 + 2 * which].wait()
        qkv_buf[which] = mm(n1, columns(attn_buf, which, which + 1)).astype(BF16)
    qkv_copy = pltpu.make_async_copy(qkv_buf, qkv_hbm, qkv_sem)
    qkv_copy.start()
    quad = 4 * size
    scale = 1.0 / math.sqrt(size)
    same = col_ref[...] == row_ref[...]

    def low_copy(j):
        part = pl.ds(j * 4, 4)
        return pltpu.make_async_copy(low_buf.at[part], low_hbm.at[part], low_sem.at[j])

    def turned_copy(j):
        part = pl.ds(j * 4, 4)
        return pltpu.make_async_copy(turned_buf.at[part], turned_hbm.at[part], turned_sem.at[j])

    def step(j, carry):
        lanes = pl.ds(pl.multiple_of(j * quad, quad), quad)
        query, keys, vals = qkv_buf[0, :, lanes], qkv_buf[1, :, lanes], qkv_buf[2, :, lanes]
        zero = jnp.zeros_like(query)
        attended = jnp.zeros((rows, quad), F32)
        for head in range(4):
            mask = head_mask((rows, quad), head, size)
            shares = softmax_shares(jnp.where(mask, query, zero), keys, same, scale)
            low = shares.astype(BF16)
            low_buf[j * 4 + head] = low
            turned_buf[j * 4 + head] = shares.T.astype(BF16)
            attended = jnp.where(mask, mm(low, vals), attended)
        att_ref[:, lanes] = attended.astype(BF16)
        low_copy(j).start()
        turned_copy(j).start()
        return carry

    lax.fori_loop(0, model // quad, step, 0)
    for copy in copies[7:]:
        copy.wait()
    mid = emb_ref[...] + mm_nt(att_ref[...], columns(attn_buf, 3, 4))
    mid_ref[...] = mid
    n2_ref[...] = (normalize(mid)[0] * gain_ref[...]).astype(BF16)
    qkv_copy.wait()
    for j in range(model // quad):
        low_copy(j).wait()
        turned_copy(j).wait()


def mlp_kernel(
    n2_hbm, og_hbm, weights_hbm, top_ref, low_ref, out_ref,
    n2_ref, og_ref, up_buf, down_buf, acc_out, acc_grad, up_sem, down_sem, sem,
):
    chunks, _, width = up_buf.shape

    def up_copy(j):
        start = pl.multiple_of(j * width, width)
        source = weights_hbm.at[:, pl.ds(start, width)]
        return pltpu.make_async_copy(source, up_buf.at[j], up_sem.at[j])

    def down_copy(j):
        start = pl.multiple_of((chunks + j) * width, width)
        source = weights_hbm.at[:, pl.ds(start, width)]
        return pltpu.make_async_copy(source, down_buf.at[j], down_sem.at[j])

    first = pltpu.make_async_copy(n2_hbm, n2_ref, sem.at[0])
    second = pltpu.make_async_copy(og_hbm, og_ref, sem.at[1])
    first.start()
    up_copy(0).start()
    second.start()
    down_copy(0).start()
    for j in range(1, chunks):
        up_copy(j).start()
        down_copy(j).start()
    acc_out[...] = jnp.zeros_like(acc_out)
    acc_grad[...] = jnp.zeros_like(acc_grad)
    first.wait()
    second.wait()

    def front(j):
        up_copy(j).wait()
        pre = mm(n2_ref[...], up_buf[j])
        down_copy(j).wait()
        return pre, mm(og_ref[...], down_buf[j])

    def back(j, pre, grad_hidden):
        root = math.sqrt(2.0 / math.pi)
        square = pre * pre
        tanh = jnp.tanh(root * pre * (1.0 + 0.044715 * square))
        half = 0.5 * (1.0 + tanh)
        act = (pre * half).astype(BF16)
        slope = half + 0.5 * pre * (1.0 - tanh * tanh) * (root * (1.0 + 3.0 * 0.044715 * square))
        grad_pre = (grad_hidden * slope).astype(BF16)
        acc_grad[...] += mm_nt(grad_pre, up_buf[j])
        acc_out[...] += mm_nt(act, down_buf[j])

    now = front(0)
    for j in range(chunks):
        later = front(j + 1) if j + 1 < chunks else None
        back(j, *now)
        now = later
    middle = top_ref.shape[0]
    top_ref[...] = acc_grad[:middle].astype(BF16)
    low_ref[...] = acc_grad[middle:].astype(BF16)
    out_ref[...] = acc_out[...].astype(BF16)


def backward_kernel(
    size, images,
    near_hbm, far_hbm,
    og_ref, mid_ref, top_mine_ref, top_theirs_ref, low_mine_ref, low_theirs_ref, qkv_buf, low_buf, turned_buf,
    emb_ref, emb_w_ref, pert_ref, gain1_ref, gain2_ref, ball_ref, col_ref,
    new_ref,
    attn_buf, acc_grad, heads_ref, proj_ref, sem,
):
    rows, model = og_ref.shape
    core = lax.rem(lax.axis_index("rows"), 2)
    head_part = pl.ds(0, 3 * model)
    out_part = pl.ds(3 * model, model)
    pairs = (
        (near_hbm.at[:, :, out_part], attn_buf.at[:, core, :, out_part]),
        (far_hbm.at[:, :, out_part], attn_buf.at[:, 1 - core, :, out_part]),
        (near_hbm.at[:, :, head_part], attn_buf.at[:, core, :, head_part]),
        (far_hbm.at[:, :, head_part], attn_buf.at[:, 1 - core, :, head_part]),
    )
    copies = [pltpu.make_async_copy(*pair, sem.at[i]) for i, pair in enumerate(pairs)]
    for copy in copies:
        copy.start()
    middle = rows // 2
    for part, mine, theirs in (
        (slice(0, middle), top_mine_ref, top_theirs_ref),
        (slice(middle, rows), low_mine_ref, low_theirs_ref),
    ):
        grad_norm_two = mine[...].astype(F32) + theirs[...].astype(F32)
        acc_grad[part] = og_ref[part].astype(F32) + norm_back(
            mid_ref[part], gain2_ref[...], grad_norm_two
        )
    grad_mid = acc_grad[...]
    for copy in copies[:2]:
        copy.wait()
    heads_ref[...] = mm(grad_mid.astype(BF16), columns(attn_buf, 3, 4)).astype(BF16)
    quad = 4 * size
    scale = 1.0 / math.sqrt(size)

    def attention_step(j, carry):
        lanes = pl.ds(pl.multiple_of(j * quad, quad), quad)
        query, keys, vals = qkv_buf[0, :, lanes], qkv_buf[1, :, lanes], qkv_buf[2, :, lanes]
        grad_heads = heads_ref[:, lanes]
        zero = jnp.zeros_like(grad_heads)
        grad_query = jnp.zeros((rows, quad), F32)
        grad_keys = jnp.zeros((rows, quad), F32)
        grad_vals = jnp.zeros((rows, quad), F32)
        for head in range(4):
            mask = head_mask((rows, quad), head, size)
            shares = low_buf[j * 4 + head].astype(F32)
            grad_shares = mm_nt(jnp.where(mask, grad_heads, zero), vals)
            grad_vals = jnp.where(mask, mm(turned_buf[j * 4 + head], grad_heads), grad_vals)
            inner = jnp.sum(grad_shares * shares, -1, keepdims=True)
            grad_scores = (shares * (grad_shares - inner) * scale).astype(BF16)
            grad_query = jnp.where(mask, mm(grad_scores, keys), grad_query)
            grad_keys = jnp.where(mask, mm_tn(grad_scores, query), grad_keys)
        for which, value in enumerate((grad_query, grad_keys, grad_vals)):
            start = pl.multiple_of(which * model + j * quad, quad)
            proj_ref[:, pl.ds(start, quad)] = value.astype(BF16)
        return carry

    lax.fori_loop(0, model // quad, attention_step, 0)
    for copy in copies[2:]:
        copy.wait()
    grad_norm = mm_nt(proj_ref[...], columns(attn_buf, 0, 3))
    grad_embed = acc_grad[...] + norm_back(emb_ref[...], gain1_ref[...], grad_norm)
    grad_input = mm_nt(grad_embed.astype(BF16), emb_w_ref[...])
    labels = col_ref[...]
    noise = pert_ref[...]
    patch = noise.shape[1]
    row_sq = jnp.sum(grad_input * grad_input, -1, keepdims=True)
    scale_rows = jnp.zeros_like(row_sq)
    counts = []
    for image in range(images):
        own = labels == image
        count = jnp.sum(jnp.where(own, 1.0, 0.0), 0, keepdims=True) * patch
        counts.append(count)
        total = jnp.sum(jnp.where(own, row_sq, 0.0), 0, keepdims=True)
        scale_rows = jnp.where(own, STEP_SIZE * lax.rsqrt(total / count + 1e-06), scale_rows)
    candidate = noise + scale_rows * grad_input
    row_sq = jnp.sum(candidate * candidate, -1, keepdims=True)
    factor_rows = jnp.zeros_like(row_sq)
    for image in range(images):
        own = labels == image
        total = jnp.sum(jnp.where(own, row_sq, 0.0), 0, keepdims=True)
        factor = jnp.minimum(
            1.0, ball_ref[:, image : image + 1] * lax.rsqrt(total / counts[image] + 1e-06)
        )
        factor_rows = jnp.where(own, factor, factor_rows)
    new_ref[...] = candidate * factor_rows


def block(*shape, dtype=BF16):
    return pltpu.VMEM(shape, dtype)


def params(mib):
    return pltpu.CompilerParams(vmem_limit_bytes=mib * MIB)


def body(
    pixels,
    perturbation,
    segment_ids,
    ball_radius,
    w_embed,
    gain_attn,
    w_qkv,
    w_out,
    gain_mlp,
    w_up,
    w_down,
    out_grad,
):
    rows, patch = pixels.shape
    model = w_embed.shape[1]
    chunk, _, share = w_qkv.shape
    units = w_up.shape[1]
    size = model // HEADS
    groups = model // share
    images = ball_radius.shape[1]

    mine = jnp.concatenate([w_qkv.reshape(chunk, 3 * share), w_out.T, w_up, w_down.T], 1)
    chunks = lax.all_gather(mine, "heads", axis=0, tiled=False)
    attn = chunks[:, :, : 4 * share].reshape(groups, chunk, 4, share)
    attn = attn.transpose(1, 2, 0, 3).reshape(chunk, 4 * model)
    half = lax.axis_index("heads") % 2
    mlp = chunks[:, :, 4 * share :].reshape(2, groups // 2, chunk, 2, units)
    mlp = lax.dynamic_index_in_dim(mlp, half, 0, keepdims=False)
    mlp = mlp.transpose(1, 2, 0, 3).reshape(chunk, groups * units)
    weights = lax.all_gather(mlp, "rows", axis=0, tiled=True)

    sites = lax.axis_size("rows") // 2
    planes = [[2 * site + core for site in range(sites)] for core in range(2)]
    copies = jnp.broadcast_to(attn[None], (sites,) + attn.shape)
    near = lax.all_to_all(copies, "rows", 0, 0, axis_index_groups=planes)
    near = near.reshape(sites * chunk, 4 * model)
    far = lax.ppermute(near, "rows", [(row, row ^ 1) for row in range(2 * sites)])

    shard = (sites, chunk, 4 * model)
    near, far = near.reshape(shard), far.reshape(shard)

    labels_col = segment_ids.reshape(rows, 1)
    labels_row = segment_ids.reshape(1, rows)
    gain1 = gain_attn.reshape(1, model)
    gain2 = gain_mlp.reshape(1, model)
    quads = model // (4 * size)
    full = lambda dt: jax.ShapeDtypeStruct((rows, model), dt)
    vmem = pl.BlockSpec(memory_space=pltpu.VMEM)
    outside = pl.BlockSpec(memory_space=pl.ANY)
    semaphores = pltpu.SemaphoreType.DMA

    embedded, normed_one = pl.pallas_call(
        embed_kernel,
        in_specs=[vmem] * 4,
        out_specs=[vmem] * 2,
        out_shape=[full(F32), full(BF16)],
        compiler_params=params(12),
        cost_estimate=pl.CostEstimate(
            flops=2 * rows * patch * model, bytes_accessed=5 * 1024 * 1024, transcendentals=0
        ),
    )(pixels, perturbation, w_embed, gain1)

    squares = jax.ShapeDtypeStruct((HEADS, rows, rows), BF16)
    qkv, low, turned, stream_mid, normed_two = pl.pallas_call(
        lambda *refs: attention_kernel(size, *refs),
        in_specs=[outside] * 4 + [vmem] * 3,
        out_specs=[outside] * 3 + [vmem] * 2,
        out_shape=[jax.ShapeDtypeStruct((3, rows, model), BF16), squares, squares]
        + [full(F32), full(BF16)],
        scratch_shapes=[
            block(rows, model),
            block(rows, model, dtype=F32),
            block(sites, 2, chunk, 4 * model),
            block(3, rows, model),
            block(HEADS, rows, rows),
            block(HEADS, rows, rows),
            block(rows, model),
            semaphores((10,)),
            semaphores((quads,)),
            semaphores((quads,)),
            semaphores,
        ],
        compiler_params=params(56),
    )(normed_one, embedded, near, far, gain2, labels_col, labels_row)

    width = 1024
    count = groups * units // 2 // width
    half_rows = jax.ShapeDtypeStruct((rows // 2, model), BF16)
    top_mine, low_mine, out_mine = pl.pallas_call(
        mlp_kernel,
        in_specs=[outside] * 3,
        out_specs=[vmem] * 3,
        out_shape=[half_rows, half_rows, full(BF16)],
        scratch_shapes=[
            block(rows, model),
            block(rows, model),
            block(count, model, width),
            block(count, model, width),
            block(rows, model, dtype=F32),
            block(rows, model, dtype=F32),
            semaphores((count,)),
            semaphores((count,)),
            semaphores((2,)),
        ],
        compiler_params=params(49),
    )(normed_two, out_grad, weights)

    down = [(group, (group - 1) % groups) for group in range(groups)]
    above = [(group, (group + 1) % groups) for group in range(groups)]
    top_theirs = lax.ppermute(top_mine, "heads", down)
    low_theirs = lax.ppermute(low_mine, "heads", above)
    out_theirs = lax.ppermute(out_mine, "heads", [(group, group ^ 1) for group in range(groups)])
    held = (out_grad, stream_mid, top_mine, top_theirs, low_mine, low_theirs)
    held = held + (qkv, low, turned, embedded, w_embed)
    held = held + (perturbation, gain1, gain2, ball_radius, labels_col)
    updated = pl.pallas_call(
        lambda *refs: backward_kernel(size, images, *refs),
        in_specs=[outside] * 2 + [vmem] * len(held),
        out_specs=vmem,
        out_shape=jax.ShapeDtypeStruct((rows, patch), F32),
        scratch_shapes=[
            block(sites, 2, chunk, 4 * model),
            block(rows, model, dtype=F32),
            block(rows, model),
            block(rows, 3 * model),
            semaphores((4,)),
        ],
        compiler_params=params(30),
        cost_estimate=pl.CostEstimate(
            flops=16 * rows * model * model, bytes_accessed=20 * 1024 * 1024, transcendentals=0
        ),
    )(near, far, *held)
    out_theirs, updated = lax.optimization_barrier((out_theirs, updated))
    block_out = stream_mid + (out_mine.astype(F32) + out_theirs.astype(F32))
    return (block_out.astype(BF16), updated)


def solution(mesh):
    in_specs = (
        P("rows", None),
        P("rows", None),
        P("rows", None),
        P("rows", None),
        P(),
        P(),
        P("rows", None, "heads"),
        P("heads", "rows"),
        P(),
        P("rows", "heads"),
        P("heads", "rows"),
        P("rows", None),
    )
    out_specs = (P("rows", None), P("rows", None))
    return jax.shard_map(body, mesh=mesh, in_specs=in_specs, out_specs=out_specs, check_vma=False)
```
